32 devices in a mesh: member: 2 (over y), seq: 16 (over z, x, core).
Axes of the slice: x: 2, y: 2, z: 4, core: 2. Of those that a mesh axis runs over, the one named last changes fastest.
Arguments:
- hidden: bfloat16 [2, 6144, 2880], P('member', 'seq'), may hold values from -6 to 6
- segments: int32 [6144], replicated, may hold values from 0 to 31, never falling along the last dimension, each value on 1 to 768 neighbouring positions
- pre_gain: float32 [2, 2880], P('member'), may hold values from 0.5 to 1.5
- w_query: bfloat16 [2, 2880, 2048], P('member', 'seq'), may hold values from -3 to 3
- w_key: bfloat16 [2, 2880, 256], P('member', 'seq'), may hold values from -3 to 3
- w_value: bfloat16 [2, 2880, 256], P('member', 'seq'), may hold values from -0.109375 to 0.109375
- w_output: bfloat16 [2, 2048, 2880], P('member', 'seq'), may hold values from -0.125 to 0.125
- post_gain: float32 [2, 2880], P('member'), may hold values from 0.5 to 1.5
- final_gain: float32 [2, 2880], P('member'), may hold values from 0.5 to 1.5
- w_judge: bfloat16 [2, 2880, 128], P('member'), may hold values from -0.21875 to 0.21875
Outputs:
- residual_out: bfloat16 [2, 6144, 2880], P('member', 'seq')
- logits: float32 [6144, 128], P('seq')
The draws below stay inside these ranges and needn't reach their ends.
Inputs may be any that keep to these rules, and one draw needn't show every extreme that they name: `segments`: segment numbers never fall from one token to the next; every number is used, each names 1 to 768 consecutive tokens, and one names exactly 768.
All inputs are finite; a program needn't handle non-finite values.
Results may differ from the reference program's by a relative error of at most 0.014.
Values may be sent and summed in bfloat16 or wider, within the bound.
No kernel may reach another device: no remote copies, remote signals or barrier semaphores. Data moves between devices by JAX's collectives and lax.ppermute only.
A program may use at most 128 MiB of HBM per device.

```python
import math
import jax
import jax.numpy as jnp
import numpy as np
from jax import lax

D = 2880
QH = 32
KVH = 4
HD = 64
WINDOW = 128
JUDGE = 128
TOK_DEV = 384
MEMBERS = 2
TOKENS = 6144
SEGMENTS = 32


def loud_groups(key):
    chosen = jax.random.randint(jax.random.fold_in(key, 5), (MEMBERS,), 0, KVH)
    strength = jax.random.uniform(jax.random.fold_in(key, 6), (MEMBERS,), jnp.float32, 4.0, 6.0)
    return (chosen, strength)


def entries(key, shape):
    return jax.random.normal(key, shape, jnp.float32)


def projection_draw(key, salt, group_of):
    chosen, strength = loud_groups(key)
    loud = group_of[None, :] == chosen[:, None]
    factor = jnp.where(loud, strength[:, None], 1.0)
    base = entries(jax.random.fold_in(key, salt), (MEMBERS, D, group_of.shape[0]))
    values = base * (1.0 / math.sqrt(D)) * factor[:, None, :]
    return jnp.clip(values, -3.0, 3.0).astype(jnp.bfloat16)


def draw_w_query(key, part):
    group_of = jnp.arange(QH * HD, dtype=jnp.int32) // HD // (QH // KVH)
    return projection_draw(key, 11, group_of)


def draw_w_key(key, part):
    group_of = jnp.arange(KVH * HD, dtype=jnp.int32) // HD
    return projection_draw(key, 13, group_of)


def level_of(own_key, extent, pieces, low, high):
    gain = 1.0
    for position, shards_of in pieces:
        draws = jax.random.uniform(jax.random.fold_in(jax.random.fold_in(own_key, 6), position), (shards_of,), jnp.float32, low / len(pieces), high / len(pieces))
        gain = gain * jnp.repeat(jnp.exp(draws), extent[position] // shards_of).reshape((-1,) + (1,) * (len(extent) - 1 - position))
    return gain


def length_profile(count, total, reach, lean):
    portions = [(1 << 20) // math.isqrt(rank ** lean) + 1 for rank in range(2, count + 1)]
    spare, holding = total - reach - (count - 1), [1] * (count - 1)
    while spare > 0:
        movable = [i for i in range(count - 1) if holding[i] < reach]
        whole, left = sum([portions[i] for i in movable]), spare
        for i in movable:
            addition = min(reach - holding[i], max(1, left * portions[i] // whole), spare)
            holding[i] = holding[i] + addition
            spare = spare - addition
    return np.array([reach] + holding)


def uneven_parts(rng, number_of, total, reach, slope):
    if number_of == 2:
        one = jax.random.randint(rng, (), max(1, total - reach), min(reach, total - 1) + 1)
        return jnp.stack([one, total - one])
    lengths = jnp.asarray(length_profile(number_of, total, reach, slope), jnp.int32)
    couples = (number_of - 1) // 2
    giver, taker = lengths[1:1 + 2 * couples:2], lengths[2:2 + 2 * couples:2]
    slack = jnp.minimum(giver - 1, reach - taker)
    moved = jax.random.randint(jax.random.fold_in(rng, 1), (couples,), 0, 1 << 20) % (slack + 1)
    lengths = lengths.at[1:1 + 2 * couples:2].set(giver - moved).at[2:2 + 2 * couples:2].set(taker + moved)
    return lengths[jax.random.permutation(jax.random.fold_in(rng, 2), number_of)]


def normal_values(own_key, dims, spread, bound, split=(), kind=jnp.bfloat16):
    values = spread * jax.random.normal(own_key, dims, jnp.float32)
    if split:
        values = values * level_of(own_key, dims, split, -0.22, 0.18)
    return jnp.clip(values, -bound, bound).astype(kind)


def setup_inputs(seed: int = 0) -> dict:
    splits = jax.random.split(jax.random.key(seed), 11)
    hidden = normal_values(splits[0], (MEMBERS, TOKENS, D), 1.0, 6.0, ((0, 2), (1, 16)))
    segments = jnp.searchsorted(jnp.cumsum(uneven_parts(splits[1], SEGMENTS, TOKENS, 2 * TOK_DEV, 2)), jnp.arange(TOKENS), side="right").astype(jnp.int32)
    pre_gain = jnp.clip(0.5 + 1.0 * jax.random.uniform(splits[2], (MEMBERS, D), jnp.float32) ** level_of(splits[2], (MEMBERS, D), ((0, 2),), -0.2, 0.2), 0.5, 1.5)
    w_query = draw_w_query(jax.random.fold_in(splits[10], 71), 0)
    w_key = draw_w_key(jax.random.fold_in(splits[10], 71), 0)
    w_value = normal_values(splits[5], (MEMBERS, D, KVH * HD), D ** -0.5, 0.109375, ((0, 2), (1, 16)))
    w_output = normal_values(splits[6], (MEMBERS, QH * HD, D), (QH * HD) ** -0.5, 0.125, ((0, 2), (1, 16)))
    post_gain = jnp.clip(0.5 + 1.0 * jax.random.uniform(splits[7], (MEMBERS, D), jnp.float32) ** level_of(splits[7], (MEMBERS, D), ((0, 2),), -0.2, 0.2), 0.5, 1.5)
    final_gain = jnp.clip(0.5 + 1.0 * jax.random.uniform(splits[8], (MEMBERS, D), jnp.float32) ** level_of(splits[8], (MEMBERS, D), ((0, 2),), -0.2, 0.2), 0.5, 1.5)
    w_judge = normal_values(splits[9], (MEMBERS, D, JUDGE), (D // 4) ** -0.5, 0.21875, ((0, 2),))
    return {"hidden": hidden, "segments": segments, "pre_gain": pre_gain, "w_query": w_query, "w_key": w_key, "w_value": w_value, "w_output": w_output, "post_gain": post_gain, "final_gain": final_gain, "w_judge": w_judge}


epsilon = 1e-06
softcap = 50.0
rope_base = 10000.0

def rms_norm(inputs, scale_gain):
    values = inputs.astype(jnp.float32)
    return values * lax.rsqrt(lax.optimization_barrier(jnp.mean(values * values, axis=-1, keepdims=True)) + epsilon) * scale_gain

def rotate(inputs, positions):
    head_size = inputs.shape[-1]
    half_dim = head_size // 2
    frequency = jnp.exp(jnp.arange(half_dim, dtype=jnp.float32) * (-2.0 * math.log(rope_base) / head_size))
    angles = positions.astype(jnp.float32)[:, None] * frequency[None, :]
    cosine_term = jnp.cos(angles)[:, None, :]
    sine_term = jnp.sin(angles)[:, None, :]
    lower_half = inputs[..., :half_dim]
    upper_half = inputs[..., half_dim:]
    return jnp.concatenate([lower_half * cosine_term - upper_half * sine_term, upper_half * cosine_term + lower_half * sine_term], axis=-1)

def attend(queries, key_rows, val_rows, seg_query, seg_key):
    query_count = queries.shape[0]
    key_count = key_rows.shape[0]
    grouped = queries.reshape(query_count, KVH, QH // KVH, HD).astype(jnp.float32)
    key_heads = key_rows.reshape(key_count, KVH, HD).astype(jnp.float32)
    scores = jnp.einsum('qhgd,khd->hgqk', grouped, key_heads)
    scores = softcap * jnp.tanh(scores / softcap)
    distance = jnp.arange(query_count)[:, None] + (key_count - query_count) - jnp.arange(key_count)[None, :]
    allowed = (distance >= 0) & (distance < WINDOW) & (seg_query[:, None] == seg_key[None, :])
    expanded = jnp.where(allowed, jnp.exp(scores), 0.0)
    weights = (expanded / lax.optimization_barrier(jnp.sum(expanded, axis=-1, keepdims=True))).astype(jnp.bfloat16)
    value_heads = val_rows.reshape(key_count, KVH, HD).astype(jnp.float32)
    result = jnp.einsum('hgqk,khd->qhgd', weights.astype(jnp.float32), value_heads)
    return result.reshape(query_count, QH * HD).astype(jnp.bfloat16)

def member_pass(member_hidden, segments, pre_gain, w_query, w_key, w_value, w_output, post_gain, final_gain, w_judge):
    tok_count = member_hidden.shape[0]
    normed = rms_norm(member_hidden, pre_gain).astype(jnp.bfloat16)
    positions = jnp.arange(tok_count, dtype=jnp.int32)
    queries = jnp.dot(normed, w_query, preferred_element_type=jnp.float32).reshape(tok_count, QH, HD)
    queries = (rotate(queries, positions) * (1.0 / math.sqrt(HD))).astype(jnp.bfloat16).reshape(tok_count, QH * HD)
    key_rows = jnp.dot(normed, w_key, preferred_element_type=jnp.float32).reshape(tok_count, KVH, HD)
    key_rows = rotate(key_rows, positions).astype(jnp.bfloat16).reshape(tok_count, KVH * HD)
    val_rows = jnp.dot(normed, w_value, preferred_element_type=jnp.float32).astype(jnp.bfloat16)
    padded_keys = jnp.concatenate([jnp.zeros((WINDOW, KVH * HD), jnp.bfloat16), key_rows], axis=0)
    padded_values = jnp.concatenate([jnp.zeros((WINDOW, KVH * HD), jnp.bfloat16), val_rows], axis=0)
    padded_segments = jnp.concatenate([jnp.full((WINDOW,), -1, jnp.int32), segments.astype(jnp.int32)], axis=0)

    def one_block(block_number):
        row_start = (block_number * WINDOW).astype(jnp.int32)
        block_queries = lax.dynamic_slice_in_dim(queries, row_start, WINDOW, 0)
        block_keys = lax.dynamic_slice_in_dim(padded_keys, row_start, 2 * WINDOW, 0)
        block_values = lax.dynamic_slice_in_dim(padded_values, row_start, 2 * WINDOW, 0)
        seg_query = lax.dynamic_slice_in_dim(segments.astype(jnp.int32), row_start, WINDOW, 0)
        seg_key = lax.dynamic_slice_in_dim(padded_segments, row_start, 2 * WINDOW, 0)
        return attend(block_queries, block_keys, block_values, seg_query, seg_key)
    attended = lax.map(one_block, jnp.arange(tok_count // WINDOW, dtype=jnp.int32))
    attended = attended.reshape(tok_count, QH * HD)
    projected = jnp.dot(attended, w_output, preferred_element_type=jnp.float32)
    updated = (member_hidden.astype(jnp.float32) + rms_norm(projected, post_gain)).astype(jnp.bfloat16)
    closing = rms_norm(updated, final_gain).astype(jnp.bfloat16)
    verdict = jnp.dot(closing, w_judge, preferred_element_type=jnp.float32)
    return (updated, verdict)

def reference(hidden, segments, pre_gain, w_query, w_key, w_value, w_output, post_gain, final_gain, w_judge):
    member_count = hidden.shape[0]
    updated_all = []
    summed = jnp.zeros((hidden.shape[1], w_judge.shape[2]), jnp.float32)
    for member in range(member_count):
        updated, verdict = member_pass(hidden[member], segments, pre_gain[member], w_query[member], w_key[member], w_value[member], w_output[member], post_gain[member], final_gain[member], w_judge[member])
        updated_all.append(updated)
        summed = summed + verdict
    return (jnp.stack(updated_all, axis=0), summed / member_count)
```

```python
import functools
import math

import jax
import jax.numpy as jnp
from jax import lax
from jax.experimental import pallas as pl
from jax.experimental.pallas import tpu as pltpu
from jax.sharding import PartitionSpec as P

QH = 32
KVH = 4
HD = 64
WINDOW = 128
CORES = 2
GROUP = 4
LANES = 128
ROWS = 128

epsilon = 1e-06
softcap = 50.0
rope_base = 10000.0
VMEM_LIMIT = 48 * 1024 * 1024


def pieces(total, step):
    return [(at, min(step, total - at)) for at in range(0, total, step)]


def accumulate(x_refs, w_refs, prior, at, size):
    total = prior
    for x_ref, w_ref in zip(x_refs, w_refs):
        x = x_ref[0] if len(x_ref.shape) == 3 else x_ref[...]
        part = jnp.dot(x, w_ref[:, at : at + size], preferred_element_type=jnp.float32)
        total = part if total is None else total + part
    return total


def rotated(block, cosine, sine):
    lane = lax.broadcasted_iota(jnp.int32, block.shape, 1)
    half = HD // 2
    other = jnp.where(
        lane % HD < half, pltpu.roll(block, LANES - half, 1), pltpu.roll(block, half, 1)
    )
    return block * cosine + other * sine


def qkv_kernel(first, last, _, *refs):
    x_refs, w_refs, refs = refs[:GROUP], refs[GROUP : 2 * GROUP], refs[2 * GROUP :]
    acc_ref = None
    if not first:
        acc_ref, refs = refs[0], refs[1:]
    if last:
        cos_ref, sin_ref, q_ref, kv_ref = refs
        q_wide, k_wide = QH * HD, KVH * HD
        cosine, sine = cos_ref[...], sin_ref[...]
    else:
        (out_ref,) = refs
    for at, size in pieces(w_refs[0].shape[1], 4 * LANES):
        prior = None if first else acc_ref[:, at : at + size]
        total = accumulate(x_refs, w_refs, prior, at, size)
        if not last:
            out_ref[:, at : at + size] = total
            continue
        for low in range(0, size, LANES):
            block = total[:, low : low + LANES]
            column = at + low
            if column < q_wide:
                block = rotated(block, cosine, sine) * (1.0 / math.sqrt(HD))
                q_ref[:, column : column + LANES] = block.astype(jnp.bfloat16)
                continue
            column = column - q_wide
            if column < k_wide:
                block = rotated(block, cosine, sine)
            kv_ref[:, column : column + LANES] = block.astype(jnp.bfloat16)


def qkv_group(indices, chunks, units, acc, tables):
    _, rows, depth = chunks.shape
    wide = units[0].shape[1]
    first, last = acc is None, tables is not None
    x_specs = [
        pl.BlockSpec((1, ROWS, depth), lambda m, ids, k=k: (ids[k], m, 0))
        for k in range(GROUP)
    ]
    w_specs = [pl.BlockSpec((depth, wide), lambda m, ids: (0, 0)) for _ in units]
    rows_spec = lambda width: pl.BlockSpec((ROWS, width), lambda m, ids: (m, 0))
    operands, specs, aliases = [chunks] * GROUP + list(units), x_specs + w_specs, {}
    if not first:
        operands.append(acc)
        specs.append(rows_spec(wide))
    if last:
        operands += list(tables)
        specs += [rows_spec(LANES)] * 2
        kv_wide = 2 * KVH * HD
        out_shape = (
            jax.ShapeDtypeStruct((rows, wide - kv_wide), jnp.bfloat16),
            jax.ShapeDtypeStruct((rows, kv_wide), jnp.bfloat16),
        )
        out_specs = (rows_spec(wide - kv_wide), rows_spec(kv_wide))
    else:
        out_shape = jax.ShapeDtypeStruct((rows, wide), jnp.float32)
        out_specs = rows_spec(wide)
        if not first:
            aliases = {1 + 2 * GROUP: 0}
    return pl.pallas_call(
        functools.partial(qkv_kernel, first, last),
        grid_spec=pltpu.PrefetchScalarGridSpec(
            num_scalar_prefetch=1, grid=(rows // ROWS,), in_specs=specs, out_specs=out_specs
        ),
        out_shape=out_shape,
        input_output_aliases=aliases,
        compiler_params=pltpu.CompilerParams(vmem_limit_bytes=VMEM_LIMIT),
        cost_estimate=pl.CostEstimate(
            flops=2 * rows * depth * wide * GROUP,
            bytes_accessed=2 * GROUP * depth * wide + 8 * rows * wide,
            transcendentals=0,
        ),
    )(indices, *operands)


def attend_kernel(q_ref, before_ref, own_ref, seg_q_ref, seg_before_ref, seg_own_ref, out_ref):
    rows = q_ref.shape[0]
    count = 2 * rows
    distance = (
        lax.broadcasted_iota(jnp.int32, (rows, count), 0)
        + rows
        - lax.broadcasted_iota(jnp.int32, (rows, count), 1)
    )
    seg_keys = jnp.concatenate([seg_before_ref[...], seg_own_ref[...]], axis=1)
    allowed = (distance >= 0) & (distance < WINDOW) & (seg_q_ref[...] == seg_keys)
    keys = jnp.concatenate([before_ref[...], own_ref[...]], axis=0)
    span = QH // KVH
    for g in range(KVH):
        key = keys[:, g * HD : (g + 1) * HD]
        value = keys[:, (KVH + g) * HD : (KVH + g + 1) * HD]
        for pair in range(span // 2):
            outs = []
            for side in range(2):
                h = g * span + 2 * pair + side
                query = q_ref[:, h * HD : (h + 1) * HD]
                scores = lax.dot_general(
                    query, key, (((1,), (1,)), ((), ())), preferred_element_type=jnp.float32
                )
                expanded = jnp.exp(softcap * jnp.tanh(scores * (1.0 / softcap)))
                expanded = jnp.where(allowed, expanded, 0.0)
                total = jnp.sum(expanded, axis=1, keepdims=True)
                mixed = jnp.dot(
                    expanded.astype(jnp.bfloat16), value, preferred_element_type=jnp.float32
                )
                outs.append(mixed / total)
            at = (g * span + 2 * pair) * HD
            out_ref[:, at : at + 2 * HD] = jnp.concatenate(outs, axis=1).astype(jnp.bfloat16)


def attend(queries, keys_values, seg_q, seg_keys):
    rows, wide = queries.shape
    kv_wide = keys_values.shape[1]
    return pl.pallas_call(
        attend_kernel,
        grid=(rows // ROWS,),
        in_specs=[
            pl.BlockSpec((ROWS, wide), lambda m: (m, 0)),
            pl.BlockSpec((ROWS, kv_wide), lambda m: (m, 0)),
            pl.BlockSpec((ROWS, kv_wide), lambda m: (m + 1, 0)),
            pl.BlockSpec((ROWS, 1), lambda m: (m, 0)),
            pl.BlockSpec((1, ROWS), lambda m: (0, m)),
            pl.BlockSpec((1, ROWS), lambda m: (0, m + 1)),
        ],
        out_specs=pl.BlockSpec((ROWS, wide), lambda m: (m, 0)),
        out_shape=jax.ShapeDtypeStruct((rows, wide), jnp.bfloat16),
        compiler_params=pltpu.CompilerParams(vmem_limit_bytes=VMEM_LIMIT),
        cost_estimate=pl.CostEstimate(
            flops=8 * rows * ROWS * wide,
            bytes_accessed=4 * rows * wide,
            transcendentals=4 * rows * ROWS * QH,
        ),
    )(queries, keys_values, keys_values, seg_q, seg_keys, seg_keys)


def out_kernel(first, last, _, *refs):
    x_refs, w_refs, refs = refs[:GROUP], refs[GROUP : 2 * GROUP], refs[2 * GROUP :]
    acc_ref = None
    if not first:
        acc_ref, refs = refs[0], refs[1:]
    if last:
        hidden_ref, post_ref, final_ref, judge_ref, updated_ref, verdict_ref, total_ref = refs
    else:
        (total_ref,) = refs
    width = w_refs[0].shape[1]
    square = None
    for at, size in pieces(width, 4 * LANES):
        prior = None if first else acc_ref[:, at : at + size]
        total = accumulate(x_refs, w_refs, prior, at, size)
        total_ref[:, at : at + size] = total
        if last:
            part = jnp.sum(total * total, axis=1, keepdims=True)
            square = part if square is None else square + part
    if not last:
        return
    scale = lax.rsqrt(square * (1.0 / width) + epsilon)
    square = None
    for at, size in pieces(width, 4 * LANES):
        cols = slice(at, at + size)
        updated = hidden_ref[:, cols].astype(jnp.float32) + (
            total_ref[:, cols] * scale * post_ref[:, cols]
        )
        updated = updated.astype(jnp.bfloat16)
        updated_ref[:, cols] = updated
        updated = updated.astype(jnp.float32)
        part = jnp.sum(updated * updated, axis=1, keepdims=True)
        square = part if square is None else square + part
    scale = lax.rsqrt(square * (1.0 / width) + epsilon)
    verdict = None
    for at, size in pieces(width, 4 * LANES):
        cols = slice(at, at + size)
        closing = updated_ref[:, cols].astype(jnp.float32) * scale * final_ref[:, cols]
        part = jnp.dot(
            closing.astype(jnp.bfloat16), judge_ref[cols, :], preferred_element_type=jnp.float32
        )
        verdict = part if verdict is None else verdict + part
    verdict_ref[...] = verdict.astype(jnp.bfloat16)


def out_group(indices, attended, units, acc, closing):
    rows = attended.shape[0]
    depth, wide = units[0].shape
    first, last = acc is None, closing is not None
    if depth % LANES:
        attended = attended.reshape(rows, -1, depth).transpose(1, 0, 2)
        x_specs = [
            pl.BlockSpec((1, ROWS, depth), lambda m, ids, k=k: (ids[k], m, 0))
            for k in range(GROUP)
        ]
    else:
        x_specs = [
            pl.BlockSpec((ROWS, depth), lambda m, ids, k=k: (m, ids[k])) for k in range(GROUP)
        ]
    w_specs = [pl.BlockSpec((depth, wide), lambda m, ids: (0, 0)) for _ in units]
    rows_spec = lambda width: pl.BlockSpec((ROWS, width), lambda m, ids: (m, 0))
    operands, specs = [attended] * GROUP + list(units), x_specs + w_specs
    aliases, scratch = {}, []
    if not first:
        operands.append(acc)
        specs.append(rows_spec(wide))
    if last:
        hidden, post_gain, final_gain, judge = closing
        operands += [hidden, post_gain, final_gain, judge]
        whole = lambda array: pl.BlockSpec(array.shape, lambda m, ids: (0, 0))
        specs += [rows_spec(wide), whole(post_gain), whole(final_gain), whole(judge)]
        out_shape = (
            jax.ShapeDtypeStruct((rows, wide), jnp.bfloat16),
            jax.ShapeDtypeStruct((rows, judge.shape[1]), jnp.bfloat16),
        )
        out_specs = (rows_spec(wide), rows_spec(judge.shape[1]))
        scratch = [pltpu.VMEM((ROWS, wide), jnp.float32)]
    else:
        out_shape = jax.ShapeDtypeStruct((rows, wide), jnp.float32)
        out_specs = rows_spec(wide)
        if not first:
            aliases = {1 + 2 * GROUP: 0}
    return pl.pallas_call(
        functools.partial(out_kernel, first, last),
        grid_spec=pltpu.PrefetchScalarGridSpec(
            num_scalar_prefetch=1,
            grid=(rows // ROWS,),
            in_specs=specs,
            out_specs=out_specs,
            scratch_shapes=scratch,
        ),
        out_shape=out_shape,
        input_output_aliases=aliases,
        compiler_params=pltpu.CompilerParams(vmem_limit_bytes=VMEM_LIMIT),
        cost_estimate=pl.CostEstimate(
            flops=2 * rows * depth * wide * GROUP,
            bytes_accessed=2 * GROUP * depth * wide + 8 * rows * wide,
            transcendentals=0,
        ),
    )(indices, *operands)


def move(block, route):
    return lax.ppermute(block, "seq", route)


class Plane:
    def __init__(self):
        self.index = lax.axis_index("seq")
        self.z = self.index // (2 * CORES)
        ends = lambda z: z in (0, 3)
        middle = lambda z: z in (1, 2)
        self.core = self.route(lambda z, x, c: (z, x, 1 - c))
        self.x_all = self.route(lambda z, x, c: (z, 1 - x, c))
        self.x_end = self.route(lambda z, x, c: (z, 1 - x, c) if ends(z) else None)
        self.x_mid = self.route(lambda z, x, c: (z, 1 - x, c) if middle(z) else None)
        self.z_pair = self.route(lambda z, x, c: (z ^ 1, x, c))
        self.z_mid = self.route(lambda z, x, c: (3 - z, x, c) if middle(z) else None)
        self.z_out = self.route(lambda z, x, c: (z ^ 1, x, c) if middle(z) else None)

    @staticmethod
    def route(target):
        route = []
        for i in range(4 * 2 * CORES):
            to = target(i // (2 * CORES), i // CORES % 2, i % CORES)
            if to is not None:
                route.append((i, (to[0] * 2 + to[1]) * CORES + to[2]))
        return route

    def gather(self, own, by_z):
        side = move(own, self.x_all)
        near = move(own, self.z_pair)
        inner = move(own, self.z_mid)
        far = move(near, self.z_mid)
        side_inner = move(side, self.z_mid)
        from_inner = move(inner, self.z_out)
        from_far = move(far, self.z_out)
        third = inner + from_inner
        fourth = far + from_far
        if by_z:
            side_near = move(near, self.x_mid) + move(side, self.z_out)
        else:
            side_near = move(near, self.x_all)
        side_third = side_inner + move(from_inner, self.x_end)
        side_fourth = move(fourth, self.x_all)
        found = [[own, side], [near, side_near], [third, side_third], [fourth, side_fourth]]
        return [pair + [move(unit, self.core) for unit in pair] for pair in found]

    def sources(self):
        i = self.index
        at_end = (self.z == 0) | (self.z == 3)
        step = 2 * CORES
        flips = [0, step, jnp.where(at_end, 2 * step, 3 * step), jnp.where(at_end, 3 * step, 2 * step)]
        return [
            jnp.stack([i ^ f, i ^ f ^ CORES, i ^ f ^ 1, i ^ f ^ CORES ^ 1]).astype(jnp.int32)
            for f in flips
        ]


def gather_whole(own):
    count = lax.axis_size("seq")
    whole = lax.all_gather(own, "seq", axis=0)
    return [[whole[i + k] for k in range(GROUP)] for i in range(0, count, GROUP)]


def body(
    structured,
    hidden, segments, pre_gain, w_query, w_key, w_value, w_output, post_gain, final_gain, w_judge,
):
    own_rows = hidden[0]
    tok_rows, width = own_rows.shape
    shards = lax.axis_size("seq")
    dev_index = lax.axis_index("seq")
    row_first = dev_index * tok_rows

    unit_in = jnp.concatenate([w_query[0], w_key[0], w_value[0]], axis=1)
    unit_out = w_output[0]
    if structured:
        plane = Plane()
        groups_in = plane.gather(unit_in, True)
        groups_out = plane.gather(unit_out, False)
        sources = plane.sources()
    else:
        groups_in, groups_out = gather_whole(unit_in), gather_whole(unit_out)
        sources = [jnp.arange(i, i + GROUP, dtype=jnp.int32) for i in range(0, shards, GROUP)]

    values = own_rows.astype(jnp.float32)
    normed = values * lax.rsqrt(jnp.mean(values * values, axis=-1, keepdims=True) + epsilon)
    normed = (normed * pre_gain[0]).astype(jnp.bfloat16)
    chunks = normed.reshape(tok_rows, shards, width // shards).transpose(1, 0, 2)

    half = HD // 2
    lane = jnp.arange(LANES, dtype=jnp.int32)
    frequency = jnp.exp((lane % half).astype(jnp.float32) * (-2.0 * math.log(rope_base) / HD))
    positions = row_first + jnp.arange(tok_rows, dtype=jnp.int32)
    angles = positions.astype(jnp.float32)[:, None] * frequency[None, :]
    tables = (jnp.cos(angles), jnp.where(lane % HD < half, -1.0, 1.0) * jnp.sin(angles))

    acc = None
    for k, (ids, units) in enumerate(zip(sources, groups_in)):
        end = k == len(sources) - 1
        acc = qkv_group(ids, chunks, units, acc, tables if end else None)
    queries, keys_values = acc

    line = [(i, i + 1) for i in range(shards - 1)]
    before = lax.ppermute(keys_values[tok_rows - WINDOW :], "seq", line)
    keys_values = jnp.concatenate([before, keys_values], axis=0)
    seg_own = lax.dynamic_slice_in_dim(segments, row_first, tok_rows, 0)
    seg_prior = lax.dynamic_slice_in_dim(segments, jnp.maximum(row_first - WINDOW, 0), WINDOW, 0)
    seg_prior = jnp.where(dev_index > 0, seg_prior, -1)
    seg_keys = jnp.concatenate([seg_prior, seg_own])[None, :]
    attended = attend(queries, keys_values, seg_own[:, None], seg_keys)

    closing = (own_rows, post_gain, final_gain, w_judge[0])
    acc = None
    for k, (ids, units) in enumerate(zip(sources, groups_out)):
        end = k == len(sources) - 1
        acc = out_group(ids, attended, units, acc, closing if end else None)
    updated, verdict = acc

    members = lax.axis_size("member")
    summed = verdict.astype(jnp.float32)
    for step in range(1, members):
        ring = [(i, (i + step) % members) for i in range(members)]
        summed = summed + lax.ppermute(verdict, "member", ring).astype(jnp.float32)
    return updated[None], summed / members


def solution(mesh):
    across = mesh.shape["member"]
    structured = across == 2 and mesh.shape["seq"] == 4 * across * CORES
    return jax.shard_map(
        functools.partial(body, structured),
        mesh=mesh,
        in_specs=(
            P("member", "seq", None),
            P(),
            P("member", None),
            P("member", "seq", None),
            P("member", "seq", None),
            P("member", "seq", None),
            P("member", "seq", None),
            P("member", None),
            P("member", None),
            P("member", None, None),
        ),
        out_specs=(P("member", "seq", None), P("seq", None)),
        check_vma=False,
    )
```

```python
import functools
import math

import jax
import jax.numpy as jnp
from jax import lax
from jax.experimental import pallas as pl
from jax.experimental.pallas import tpu as pltpu
from jax.sharding import PartitionSpec as P

QH = 32
KVH = 4
HD = 64
WINDOW = 128
CORES = 2
LANES = 128

epsilon = 1e-06
softcap = 50.0
rope_base = 10000.0
VMEM_LIMIT = 50 * 1024 * 1024


def from_behind(block, axis, distance):
    devices = range(lax.axis_size(axis))
    route = [(i - distance, i) for i in devices if i - distance in devices]
    return lax.ppermute(block, axis, route)


def rms_norm(inputs, scale_gain):
    values = inputs.astype(jnp.float32)
    return (
        values * lax.rsqrt(jnp.mean(values * values, axis=-1, keepdims=True) + epsilon) * scale_gain
    )


def rotate(inputs, positions):
    head_size = inputs.shape[-1]
    half_dim = head_size // 2
    frequency = jnp.exp(
        jnp.arange(half_dim, dtype=jnp.float32) * (-2.0 * math.log(rope_base) / head_size)
    )
    angles = positions.astype(jnp.float32)[:, None] * frequency[None, :]
    cosine_term = jnp.cos(angles)[:, None, :]
    sine_term = jnp.sin(angles)[:, None, :]
    lower_half = inputs[..., :half_dim]
    upper_half = inputs[..., half_dim:]
    return jnp.concatenate(
        [
            lower_half * cosine_term - upper_half * sine_term,
            upper_half * cosine_term + lower_half * sine_term,
        ],
        axis=-1,
    )


def attend_heads(block_queries, block_keys, block_values, seg_query, seg_key):
    query_count = block_queries.shape[0]
    key_count = block_keys.shape[0]
    head_span = QH // KVH * HD
    distance = (
        jnp.arange(query_count, dtype=jnp.int32)[:, None]
        + (key_count - query_count)
        - jnp.arange(key_count, dtype=jnp.int32)[None, :]
    )
    allowed = (distance >= 0) & (distance < WINDOW) & (seg_query[:, None] == seg_key[None, :])

    def one_head(head_index):
        query_head = lax.dynamic_slice_in_dim(
            block_queries, head_index * head_span, head_span, 1
        ).reshape(query_count, QH // KVH, HD)
        key_head = lax.dynamic_slice_in_dim(block_keys, head_index * HD, HD, 1)
        value_head = lax.dynamic_slice_in_dim(block_values, head_index * HD, HD, 1)
        scores = jnp.einsum("qgd,kd->gqk", query_head, key_head, preferred_element_type=jnp.float32)
        scores = softcap * jnp.tanh(scores / softcap)
        expanded = jnp.where(allowed[None], jnp.exp(scores), 0.0)
        weights = (expanded / jnp.sum(expanded, axis=-1, keepdims=True)).astype(jnp.bfloat16)
        head_out = jnp.einsum(
            "gqk,kd->qgd", weights, value_head, preferred_element_type=jnp.float32
        )
        return head_out.astype(jnp.bfloat16).reshape(query_count, head_span)

    per_head = lax.map(one_head, jnp.arange(KVH, dtype=jnp.int32))
    return per_head.transpose(1, 0, 2).reshape(query_count, KVH * head_span)


def gathered_body(
    hidden, segments, pre_gain, w_query, w_key, w_value, w_output, post_gain, final_gain, w_judge
):
    tok_rows = hidden.shape[1]
    dev_index = lax.axis_index("seq")
    row_first = dev_index * tok_rows
    own_rows = hidden[0]
    normed = rms_norm(own_rows, pre_gain[0]).astype(jnp.bfloat16)
    earlier = from_behind(normed[tok_rows - WINDOW :], "seq", 1)
    kv_input = jnp.concatenate([earlier, normed], axis=0)
    kv_count = kv_input.shape[0]
    queries = jnp.dot(
        normed,
        lax.all_gather(w_query[0], "seq", axis=0, tiled=True),
        preferred_element_type=jnp.float32,
    )
    key_rows = jnp.dot(
        kv_input,
        lax.all_gather(w_key[0], "seq", axis=0, tiled=True),
        preferred_element_type=jnp.float32,
    )
    val_rows = jnp.dot(
        kv_input,
        lax.all_gather(w_value[0], "seq", axis=0, tiled=True),
        preferred_element_type=jnp.float32,
    )
    query_positions = row_first + jnp.arange(tok_rows, dtype=jnp.int32)
    key_positions = row_first - (kv_count - tok_rows) + jnp.arange(kv_count, dtype=jnp.int32)
    queries = (
        (rotate(queries.reshape(tok_rows, QH, HD), query_positions) * (1.0 / math.sqrt(HD)))
        .astype(jnp.bfloat16)
        .reshape(tok_rows, QH * HD)
    )
    key_rows = (
        rotate(key_rows.reshape(kv_count, KVH, HD), key_positions)
        .astype(jnp.bfloat16)
        .reshape(kv_count, KVH * HD)
    )
    val_rows = val_rows.astype(jnp.bfloat16)
    seg_own = lax.dynamic_slice_in_dim(segments, row_first, tok_rows, 0)
    seg_prior = lax.dynamic_slice_in_dim(segments, jnp.maximum(row_first - WINDOW, 0), WINDOW, 0)
    seg_prior = jnp.where(dev_index > 0, seg_prior, -1)
    seg_keys = jnp.concatenate([seg_prior, seg_own], axis=0)
    block_rows = min(tok_rows, 512)

    def one_block(block_number):
        return attend_heads(queries, key_rows, val_rows, seg_own, seg_keys)

    attended = lax.map(one_block, jnp.arange(tok_rows // block_rows, dtype=jnp.int32)).reshape(
        tok_rows, QH * HD
    )
    projected = jnp.dot(
        attended,
        lax.all_gather(w_output[0], "seq", axis=0, tiled=True),
        preferred_element_type=jnp.float32,
    )
    updated = (own_rows.astype(jnp.float32) + rms_norm(projected, post_gain[0])).astype(
        jnp.bfloat16
    )
    closing = rms_norm(updated, final_gain[0]).astype(jnp.bfloat16)
    verdict = jnp.dot(closing, w_judge[0], preferred_element_type=jnp.float32)
    summed_verdict = lax.psum(verdict.astype(jnp.bfloat16), "member").astype(jnp.float32)
    return (updated[None], summed_verdict / lax.axis_size("member"))


def tied(value, *others):
    return lax.optimization_barrier((value, *others))[0]


def call(kernel, out_shape, *, flops=0, moved=0, transcendentals=0, **spec):
    return pl.pallas_call(
        kernel,
        out_shape=out_shape,
        compiler_params=pltpu.CompilerParams(vmem_limit_bytes=VMEM_LIMIT),
        cost_estimate=pl.CostEstimate(
            flops=1000, bytes_accessed=1000, transcendentals=0
        ),
        **spec,
    )


def scalars(count, grid, in_specs, out_specs, scratch=()):
    return dict(
        grid_spec=pltpu.PrefetchScalarGridSpec(
            num_scalar_prefetch=count,
            grid=grid,
            in_specs=in_specs,
            out_specs=out_specs,
            scratch_shapes=scratch,
        )
    )


def halves_kernel(core_ref, q_ref, k_ref, v_ref, mine_ref, other_ref):
    def write(out_ref, core):
        at = 0
        for low in range(core * LANES, q_ref.shape[1], CORES * LANES):
            out_ref[:, at : at + LANES] = q_ref[:, low : low + LANES]
            at += LANES
        for ref in (k_ref, v_ref):
            size = ref.shape[1] // CORES
            out_ref[:, at : at + size] = ref[:, core * size : (core + 1) * size]
            at += size

    for core in range(CORES):

        @pl.when(core_ref[0] == core)
        def _(core=core):
            write(mine_ref, core)
            write(other_ref, 1 - core)


def halves(core, w_query, w_key, w_value):
    rows = w_query.shape[0]
    wide = (w_query.shape[1] + w_key.shape[1] + w_value.shape[1]) // CORES
    whole = lambda array: pl.BlockSpec(array.shape, lambda m, c: (0, 0))
    half = jax.ShapeDtypeStruct((rows, wide), w_query.dtype)
    ins = (w_query, w_key, w_value)
    return call(
        halves_kernel, (half, half), moved=8 * rows * wide,
        **scalars(1, (1,), [whole(a) for a in ins], (whole(half), whole(half))),
    )(core, *ins)


def prepare_kernel(core_ref, own_ref, mate_ref, gain_ref, chunks_ref):
    count, _, depth = chunks_ref.shape
    own = pl.program_id(0) == core_ref[0]

    def write(hidden_ref):
        values = hidden_ref[...].astype(jnp.float32)
        mean = jnp.sum(values * values, axis=0, keepdims=True) * (1.0 / values.shape[0])
        scale = lax.rsqrt(mean + epsilon)
        for j in range(count):
            part = slice(j * depth, (j + 1) * depth)
            normed = hidden_ref[part, :].astype(jnp.float32) * scale * gain_ref[part, :]
            chunks_ref[j] = normed.T.astype(jnp.bfloat16)

    pl.when(own)(lambda: write(own_ref))
    pl.when(jnp.logical_not(own))(lambda: write(mate_ref))


def prepare(core, own, mate, gain, count):
    width, rows = own.shape
    depth = width // count
    whole = lambda array: pl.BlockSpec(array.shape, lambda m, c: (0, 0))
    return call(
        prepare_kernel,
        jax.ShapeDtypeStruct((count, CORES * rows, depth), jnp.bfloat16),
        flops=10 * rows * width,
        moved=10 * rows * width,
        **scalars(
            1, (CORES,), [whole(own), whole(mate), whole(gain)],
            pl.BlockSpec((count, rows, depth), lambda m, c: (0, m, 0)),
        ),
    )(core, own, mate, gain)


def rotated(block, cosine, sine):
    lane = lax.broadcasted_iota(jnp.int32, block.shape, 1)
    half = HD // 2
    other = jnp.where(
        lane % HD < half, pltpu.roll(block, LANES - half, 1), pltpu.roll(block, half, 1)
    )
    return block * cosine + other * sine


def qkv_kernel(shape, first, last, _, *refs):
    refs = list(refs)
    take = lambda: refs.pop(0)
    x_refs = [[take() for _ in range(CORES)] for _ in shape]
    total = None
    w_refs = [[[take() for _ in range(CORES)] for _ in range(n)] for n in shape]
    if not first:
        total = take()[...]
    for x_pair, parts in zip(x_refs, w_refs):
        for side in range(CORES):
            w = parts[0][side][...]
            for extra in parts[1:]:
                w = w + extra[side][...]
            part = jnp.dot(x_pair[side][0], w, preferred_element_type=jnp.float32)
            total = part if total is None else total + part
    if not last:
        take()[...] = total
        return
    cosine, sine = take()[...], take()[...]
    out_ref = take()
    width = out_ref.shape[1]
    lanes = lambda low: slice(low, low + LANES)
    keys = KVH * HD // CORES
    is_query = pl.program_id(0) < pl.num_programs(0) - 1

    @pl.when(is_query)
    def _():
        for low in range(0, width, LANES):
            block = rotated(total[:, lanes(low)], cosine, sine) * (1.0 / math.sqrt(HD))
            out_ref[:, lanes(low)] = block.astype(jnp.bfloat16)

    @pl.when(jnp.logical_not(is_query))
    def _():
        for low in range(0, width, LANES):
            block = total[:, lanes(low)]
            if low < keys:
                block = rotated(block, cosine, sine)
            out_ref[:, lanes(low)] = block.astype(jnp.bfloat16)


def qkv_group(indices, chunks, units, acc, tables):
    _, rows, depth = chunks.shape
    wide = units[0][0].shape[1] // CORES
    step = 2 * KVH * HD // CORES
    steps = wide // step
    first, last = acc is None, tables is not None
    specs, operands = [], []
    for k in range(len(units)):
        for side in range(CORES):
            specs.append(
                pl.BlockSpec(
                    (1, rows, depth), lambda n, ids, k=k, side=side: (ids[k] ^ side, 0, 0)
                )
            )
            operands.append(chunks)
    for unit in units:
        for part in unit:
            for side in range(CORES):
                specs.append(
                    pl.BlockSpec((depth, step), lambda n, ids, side=side: (0, n + side * steps))
                )
                operands.append(part)
    block = pl.BlockSpec((rows, step), lambda n, ids: (0, n))
    if not first:
        operands.append(acc)
        specs.append(block)
    if last:
        operands += list(tables)
        specs += [pl.BlockSpec((rows, LANES), lambda n, ids: (0, 0))] * 2
    return call(
        functools.partial(qkv_kernel, [len(unit) for unit in units], first, last),
        jax.ShapeDtypeStruct((rows, wide), jnp.bfloat16 if last else jnp.float32),
        flops=2 * rows * depth * wide * len(units) * CORES,
        moved=4 * len(units) * depth * wide + 8 * rows * wide,
        **scalars(1, (steps,), specs, block),
    )(indices, *operands)


def attend_kernel(core_ref, q_ref, own0_ref, own1_ref, mate0_ref, mate1_ref, seg_q_ref, seg0_ref, seg1_ref, *out_refs):
    out_ref = out_refs[-1]
    rows = q_ref.shape[0]
    count = 2 * rows
    distance = (
        lax.broadcasted_iota(jnp.int32, (count, rows), 1)
        + rows
        - lax.broadcasted_iota(jnp.int32, (count, rows), 0)
    )
    seg_keys = jnp.concatenate([seg0_ref[...], seg1_ref[...]], axis=0)
    allowed = (distance >= 0) & (distance < WINDOW) & (seg_q_ref[...] == seg_keys)
    bias = jnp.where(allowed, 0.0, -1e9)
    own = jnp.concatenate([own0_ref[...], own1_ref[...]], axis=0).astype(jnp.float32)
    mate = jnp.concatenate([mate0_ref[...], mate1_ref[...]], axis=0).astype(jnp.float32)
    is_first = core_ref[0] == 0
    part = KVH // CORES
    sides = [jnp.where(is_first, own, mate), jnp.where(is_first, mate, own)]
    span = QH // KVH // CORES
    for g in range(KVH):
        side, at = sides[g // part], g % part * HD
        key = side[:, at : at + HD].astype(jnp.bfloat16)
        at += part * HD
        value_t = side[:, at : at + HD].T.astype(jnp.bfloat16)
        heads = range(g * span, (g + 1) * span)
        query = jnp.concatenate([q_ref[:, h * HD : (h + 1) * HD] for h in heads], axis=0)
        scores = lax.dot_general(
            key, query, (((1,), (1,)), ((), ())), preferred_element_type=jnp.float32
        )
        parts, totals = [], []
        for k in range(span):
            score = jnp.tanh(scores[:, k * rows : (k + 1) * rows] * (1.0 / softcap))
            expanded = jnp.exp2(score * (softcap / math.log(2.0)) + bias)
            totals.append(jnp.sum(expanded, axis=0, keepdims=True))
            parts.append(expanded.astype(jnp.bfloat16))
        mixed = jnp.dot(
            value_t, jnp.concatenate(parts, axis=1), preferred_element_type=jnp.float32
        )
        for k, h in enumerate(heads):
            result = mixed[:, k * rows : (k + 1) * rows] / totals[k]
            out_ref[h * HD : (h + 1) * HD, :] = result.astype(jnp.bfloat16)


def attend(core, qkv, own, mate, halo, seg_q, seg_keys, prior):
    rows = qkv.shape[0]
    q_wide = QH * HD // CORES
    kv_wide = own.shape[1]
    start = 1 if prior is None else 0
    keys = lambda ahead, column: pl.BlockSpec(
        (WINDOW, kv_wide), lambda m, c: (m + ahead, column)
    )
    segs = lambda ahead: pl.BlockSpec((WINDOW, 1), lambda m, c: (m + start + ahead, 0))
    if prior is None:
        operands = [own, own, mate, mate]
        specs = [keys(0, 0), keys(1, 0), keys(0, 0), keys(1, 0)]
        steps = rows // WINDOW - 1
    else:
        operands = [halo, own, halo, mate]
        specs = [keys(0, 0), keys(0, 0), keys(0, 1), keys(0, 0)]
        steps = 1
    specs = [
        pl.BlockSpec((WINDOW, q_wide), lambda m, c: (m + start, 0)),
        *specs,
        pl.BlockSpec((1, WINDOW), lambda m, c: (0, m + start)),
        segs(0), segs(1),
    ]
    operands = [qkv, *operands, seg_q, seg_keys, seg_keys]
    aliases = {}
    if prior is not None:
        operands.append(prior)
        specs.append(pl.BlockSpec(memory_space=pl.ANY))
        aliases = {len(operands): 0}
    return call(
        attend_kernel,
        jax.ShapeDtypeStruct((q_wide, rows), jnp.bfloat16),
        flops=8 * steps * WINDOW * WINDOW * q_wide,
        moved=4 * steps * WINDOW * q_wide,
        transcendentals=4 * steps * WINDOW * WINDOW * QH // CORES,
        input_output_aliases=aliases,
        **scalars(
            1, (steps,), specs, pl.BlockSpec((q_wide, WINDOW), lambda m, c: (0, m + start))
        ),
    )(core, *operands)


def out_kernel(shape, _, *refs):
    refs = list(refs)
    take = lambda: refs.pop(0)
    x = jnp.concatenate([take()[0] for _ in shape], axis=0)
    units = []
    for n in shape:
        w = take()[...]
        for _ in range(n - 1):
            w = w + take()[...]
        units.append(w)
    out_ref = take()
    total = jnp.dot(jnp.concatenate(units, axis=1), x, preferred_element_type=jnp.float32)
    out_ref[...] = total.astype(out_ref.dtype)


def project(indices, attended, units, dtype):
    _, depth, rows = attended.shape
    wide = units[0][0].shape[0]
    step, half, count = wide // 5, rows // CORES, len(units)
    specs = [
        pl.BlockSpec((1, depth, half), lambda m, ids, k=k: (ids[k], 0, ids[count]))
        for k in range(count)
    ]
    operands = [attended] * count
    for unit in units:
        operands += unit
        specs += [pl.BlockSpec((step, depth), lambda m, ids: (m, 0))] * len(unit)
    return call(
        functools.partial(out_kernel, [len(unit) for unit in units]),
        jax.ShapeDtypeStruct((wide, half), dtype),
        flops=2 * half * depth * wide * count,
        moved=2 * count * depth * wide + 4 * half * wide,
        **scalars(1, (wide // step,), specs, pl.BlockSpec((step, half), lambda m, ids: (m, 0))),
    )(indices, *operands)


def close_kernel(own_ref, mate_ref, hidden_ref, gains_ref, judge_ref, updated_ref, verdict_ref, total_ref):
    width = total_ref.shape[0]
    step = width // 5
    parts = [slice(low, low + step) for low in range(0, width, step)]
    square = None
    for rows in parts:
        total = own_ref[rows, :] + mate_ref[rows, :].astype(jnp.float32)
        total_ref[rows, :] = total
        part = jnp.sum(total * total, axis=0, keepdims=True)
        square = part if square is None else square + part
    scale = lax.rsqrt(square * (1.0 / width) + epsilon)
    square = None
    for rows in parts:
        updated = hidden_ref[rows, :].astype(jnp.float32) + (
            total_ref[rows, :] * scale * gains_ref[rows, 1:2]
        )
        updated = updated.astype(jnp.bfloat16)
        updated_ref[rows, :] = updated
        updated = updated.astype(jnp.float32)
        part = jnp.sum(updated * updated, axis=0, keepdims=True)
        square = part if square is None else square + part
    scale = lax.rsqrt(square * (1.0 / width) + epsilon)
    closing = updated_ref[...].astype(jnp.float32) * scale * gains_ref[:, 2:3]
    verdict = jnp.dot(
        judge_ref[...], closing.astype(jnp.bfloat16), preferred_element_type=jnp.float32
    )
    verdict_ref[...] = verdict.T.astype(jnp.bfloat16)


def close(own, mate, hidden, gains, judge):
    width, half = own.shape
    return call(
        close_kernel,
        (
            jax.ShapeDtypeStruct((width, half), jnp.bfloat16),
            jax.ShapeDtypeStruct((half, judge.shape[0]), jnp.bfloat16),
        ),
        flops=2 * width * half * judge.shape[0],
        moved=12 * width * half,
        grid=(1,),
        scratch_shapes=[pltpu.VMEM((width, half), jnp.float32)],
    )(own, mate, hidden, gains, judge)


def move(block, route):
    return lax.ppermute(block, "seq", route)


class Plane:
    def __init__(self):
        index = lax.axis_index("seq")
        self.core, self.chip = index % CORES, index // CORES
        self.z = self.chip // 2
        ends = lambda z: z in (0, 3)
        middle = lambda z: z in (1, 2)
        self.mate = self.route(lambda z, x, c: (z, x, 1 - c))
        self.x_all = self.route(lambda z, x, c: (z, 1 - x, c))
        self.x_end = self.route(lambda z, x, c: (z, 1 - x, c) if ends(z) else None)
        self.x_mid = self.route(lambda z, x, c: (z, 1 - x, c) if middle(z) else None)
        self.z_pair = self.route(lambda z, x, c: (z ^ 1, x, c))
        self.z_mid = self.route(lambda z, x, c: (3 - z, x, c) if middle(z) else None)
        self.z_out = self.route(lambda z, x, c: (z ^ 1, x, c) if middle(z) else None)
        self.line = [(i, i + CORES) for i in range(4 * 2 * CORES - CORES)]

    @staticmethod
    def route(target):
        route = []
        for i in range(4 * 2 * CORES):
            to = target(i // (2 * CORES), i // CORES % 2, i % CORES)
            if to is not None:
                route.append((i, (to[0] * 2 + to[1]) * CORES + to[2]))
        return route

    def sources(self):
        at_end = (self.z == 0) | (self.z == 3)
        flips = [0, 2, jnp.where(at_end, 4, 6), jnp.where(at_end, 6, 4)]
        return [jnp.stack([self.chip ^ f, self.chip ^ f ^ 1]).astype(jnp.int32) for f in flips]


def planned_body(
    hidden, segments, pre_gain, w_query, w_key, w_value, w_output, post_gain, final_gain, w_judge
):
    p = Plane()
    ids = p.sources()
    join = lambda *groups: jnp.concatenate([ids[g] for g in groups])
    core = p.core.astype(jnp.int32)[None]
    hidden_t = hidden[0].T
    width, tok_rows = hidden_t.shape
    shards = lax.axis_size("seq")
    chip_rows = CORES * tok_rows
    row_first = p.chip * chip_rows
    unit_out = w_output[0].T

    mine, other = halves(core, w_query[0], w_key[0], w_value[0])
    unit_in = jnp.concatenate([mine, move(other, p.mate)], axis=1)
    a_side = move(unit_in, p.x_all)
    a_near = move(unit_in, p.z_pair)
    a_inner = move(unit_in, p.z_mid)

    gains = jnp.concatenate([pre_gain, post_gain, final_gain], axis=0).T
    judge_t = w_judge[0].T
    half = HD // 2
    lane = jnp.arange(LANES, dtype=jnp.int32)
    frequency = jnp.exp((lane % half).astype(jnp.float32) * (-2.0 * math.log(rope_base) / HD))
    positions = row_first + jnp.arange(chip_rows, dtype=jnp.int32)
    angles = positions.astype(jnp.float32)[:, None] * frequency[None, :]
    tables = (jnp.cos(angles), jnp.where(lane % HD < half, -1.0, 1.0) * jnp.sin(angles))
    seg_own = lax.dynamic_slice_in_dim(segments, row_first, chip_rows, 0)
    seg_prior = lax.dynamic_slice_in_dim(segments, jnp.maximum(row_first - WINDOW, 0), WINDOW, 0)
    seg_prior = jnp.where(p.chip > 0, seg_prior, -1)
    seg_keys = jnp.concatenate([seg_prior, seg_own])[:, None]
    seg_q = seg_own[None, :]
    chunks = prepare(core, hidden_t, move(tied(hidden_t, unit_in), p.mate), gains[:, :1], shards)
    chunks, judge_t, seg_q, seg_keys, *tables = lax.optimization_barrier(
        (chunks, judge_t, seg_q, seg_keys, *tables)
    )

    a_side_near = move(tied(a_near, a_side, chunks), p.x_all)
    a_far = move(tied(a_near, a_side, chunks), p.z_mid)
    a_from_inner = move(tied(a_inner, a_side, chunks), p.z_out)

    o_near = move(tied(unit_out, a_from_inner), p.z_pair)
    o_inner = move(tied(unit_out, a_far), p.z_mid)
    a_x_third = move(a_from_inner, p.x_end)
    a_x_far = move(a_far, p.x_mid)
    a_side_inner = move(tied(a_side, a_far), p.z_mid)
    a_from_far = move(tied(a_far, a_from_inner), p.z_out)
    o_side = move(tied(unit_out, a_side_near), p.x_all)
    units = [[unit_in], [a_side], [a_near], [a_side_near]]
    acc = qkv_group(CORES * join(0, 1) + p.core, chunks, units, None, None)

    a_x_fourth = move(tied(a_from_far, acc, o_near, o_inner, o_side, a_x_third, a_x_far, a_side_inner), p.x_end)
    o_far = move(tied(o_near, acc), p.z_mid)
    o_from_inner = move(tied(o_inner, acc), p.z_out)
    units = [[a_inner, a_from_inner], [a_side_inner, a_x_third]]
    acc = qkv_group(CORES * join(2) + p.core, chunks, units, acc, None)

    o_x_third = move(tied(o_from_inner, a_x_fourth, acc), p.x_end)
    o_x_near = move(tied(o_near, a_x_far, acc), p.x_mid)
    o_from_far = move(tied(o_far, a_x_fourth, acc), p.z_out)
    o_side_inner = move(tied(o_side, o_far, acc), p.z_mid)
    units = [[a_far, a_from_far], [a_x_far, a_x_fourth]]
    qkv = qkv_group(CORES * join(3) + p.core, chunks, units, acc, tables)

    o_x_far = move(tied(o_far, o_x_near, qkv), p.x_mid)
    o_x_fourth = move(tied(o_from_far, o_x_third, qkv), p.x_end)
    o_z_side = move(tied(o_side, o_from_far, qkv), p.z_out)
    own_kv = qkv[:, QH * HD // CORES :]
    mate_kv = move(tied(own_kv, o_x_third, o_x_near, o_from_far, o_side_inner), p.mate)
    halo = jnp.concatenate([own_kv, mate_kv], axis=1)[chip_rows - WINDOW :]
    halo = move(halo, p.line)
    attended = attend(core, qkv, own_kv, mate_kv, None, seg_q, seg_keys, None)
    attended = attend(core, qkv, own_kv, mate_kv, halo, seg_q, seg_keys, attended)
    attended = attended.reshape(shards // CORES, -1, chip_rows)

    units = [[unit_out], [o_side], [o_near], [o_x_near, o_z_side]]
    units += [[o_inner, o_from_inner], [o_side_inner, o_x_third]]
    units += [[o_far, o_from_far], [o_x_far, o_x_fourth]]
    order = join(0, 1, 2, 3)
    mate = project(jnp.concatenate([order, 1 - core]), attended, units, jnp.bfloat16)
    own = project(jnp.concatenate([order, core]), attended, units, jnp.float32)
    updated, verdict = close(own, move(mate, p.mate), hidden_t, gains, judge_t)

    members = lax.axis_size("member")
    summed = verdict.astype(jnp.float32)
    for step in range(1, members):
        ring = [(i, (i + step) % members) for i in range(members)]
        summed = summed + lax.ppermute(verdict, "member", ring).astype(jnp.float32)
    return updated.T[None], summed / members


def solution(mesh):
    across = mesh.shape["member"]
    planned = across == 2 and mesh.shape["seq"] == 4 * across * CORES
    return jax.shard_map(
        planned_body if planned else gathered_body,
        mesh=mesh,
        in_specs=(
            P("member", "seq", None),
            P(),
            P("member", None),
            P("member", "seq", None),
            P("member", "seq", None),
            P("member", "seq", None),
            P("member", "seq", None),
            P("member", None),
            P("member", None),
            P("member", None, None),
        ),
        out_specs=(P("member", "seq", None), P("seq", None)),
        check_vma=False,
    )
```

```python
import functools
import math

import jax
import jax.numpy as jnp
from jax import lax
from jax.experimental import pallas as pl
from jax.experimental.pallas import tpu as pltpu
from jax.sharding import PartitionSpec as P

QH = 32
KVH = 4
HD = 64
WINDOW = 128
CORES = 2
LANES = 128

epsilon = 1e-06
softcap = 50.0
rope_base = 10000.0
MIB = 1024 * 1024


def from_behind(block, axis, distance):
    devices = range(lax.axis_size(axis))
    route = [(i - distance, i) for i in devices if i - distance in devices]
    return lax.ppermute(block, axis, route)


def rms_norm(inputs, scale_gain):
    values = inputs.astype(jnp.float32)
    return (
        values * lax.rsqrt(jnp.mean(values * values, axis=-1, keepdims=True) + epsilon) * scale_gain
    )


def rotate(inputs, positions):
    head_size = inputs.shape[-1]
    half_dim = head_size // 2
    frequency = jnp.exp(
        jnp.arange(half_dim, dtype=jnp.float32) * (-2.0 * math.log(rope_base) / head_size)
    )
    angles = positions.astype(jnp.float32)[:, None] * frequency[None, :]
    cosine_term = jnp.cos(angles)[:, None, :]
    sine_term = jnp.sin(angles)[:, None, :]
    lower_half = inputs[..., :half_dim]
    upper_half = inputs[..., half_dim:]
    return jnp.concatenate(
        [
            lower_half * cosine_term - upper_half * sine_term,
            upper_half * cosine_term + lower_half * sine_term,
        ],
        axis=-1,
    )


def attend_heads(block_queries, block_keys, block_values, seg_query, seg_key):
    query_count = block_queries.shape[0]
    key_count = block_keys.shape[0]
    head_span = QH // KVH * HD
    distance = (
        jnp.arange(query_count, dtype=jnp.int32)[:, None]
        + (key_count - query_count)
        - jnp.arange(key_count, dtype=jnp.int32)[None, :]
    )
    allowed = (distance >= 0) & (distance < WINDOW) & (seg_query[:, None] == seg_key[None, :])

    def one_head(head_index):
        query_head = lax.dynamic_slice_in_dim(
            block_queries, head_index * head_span, head_span, 1
        ).reshape(query_count, QH // KVH, HD)
        key_head = lax.dynamic_slice_in_dim(block_keys, head_index * HD, HD, 1)
        value_head = lax.dynamic_slice_in_dim(block_values, head_index * HD, HD, 1)
        scores = jnp.einsum("qgd,kd->gqk", query_head, key_head, preferred_element_type=jnp.float32)
        scores = softcap * jnp.tanh(scores / softcap)
        expanded = jnp.where(allowed[None], jnp.exp(scores), 0.0)
        weights = (expanded / jnp.sum(expanded, axis=-1, keepdims=True)).astype(jnp.bfloat16)
        head_out = jnp.einsum(
            "gqk,kd->qgd", weights, value_head, preferred_element_type=jnp.float32
        )
        return head_out.astype(jnp.bfloat16).reshape(query_count, head_span)

    per_head = lax.map(one_head, jnp.arange(KVH, dtype=jnp.int32))
    return per_head.transpose(1, 0, 2).reshape(query_count, KVH * head_span)


def gathered_body(
    hidden, segments, pre_gain, w_query, w_key, w_value, w_output, post_gain, final_gain, w_judge
):
    tok_rows = hidden.shape[1]
    dev_index = lax.axis_index("seq")
    row_first = dev_index * tok_rows
    own_rows = hidden[0]
    normed = rms_norm(own_rows, pre_gain[0]).astype(jnp.bfloat16)
    earlier = from_behind(normed[tok_rows - WINDOW :], "seq", 1)
    kv_input = jnp.concatenate([earlier, normed], axis=0)
    kv_count = kv_input.shape[0]
    queries = jnp.dot(
        normed,
        lax.all_gather(w_query[0], "seq", axis=0, tiled=True),
        preferred_element_type=jnp.float32,
    )
    key_rows = jnp.dot(
        kv_input,
        lax.all_gather(w_key[0], "seq", axis=0, tiled=True),
        preferred_element_type=jnp.float32,
    )
    val_rows = jnp.dot(
        kv_input,
        lax.all_gather(w_value[0], "seq", axis=0, tiled=True),
        preferred_element_type=jnp.float32,
    )
    query_positions = row_first + jnp.arange(tok_rows, dtype=jnp.int32)
    key_positions = row_first - (kv_count - tok_rows) + jnp.arange(kv_count, dtype=jnp.int32)
    queries = (
        (rotate(queries.reshape(tok_rows, QH, HD), query_positions) * (1.0 / math.sqrt(HD)))
        .astype(jnp.bfloat16)
        .reshape(tok_rows, QH * HD)
    )
    key_rows = (
        rotate(key_rows.reshape(kv_count, KVH, HD), key_positions)
        .astype(jnp.bfloat16)
        .reshape(kv_count, KVH * HD)
    )
    val_rows = val_rows.astype(jnp.bfloat16)
    seg_own = lax.dynamic_slice_in_dim(segments, row_first, tok_rows, 0)
    seg_prior = lax.dynamic_slice_in_dim(segments, jnp.maximum(row_first - WINDOW, 0), WINDOW, 0)
    seg_prior = jnp.where(dev_index > 0, seg_prior, -1)
    seg_keys = jnp.concatenate([seg_prior, seg_own], axis=0)
    block_rows = min(tok_rows, 512)

    def one_block(block_number):
        return attend_heads(queries, key_rows, val_rows, seg_own, seg_keys)

    attended = lax.map(one_block, jnp.arange(tok_rows // block_rows, dtype=jnp.int32)).reshape(
        tok_rows, QH * HD
    )
    projected = jnp.dot(
        attended,
        lax.all_gather(w_output[0], "seq", axis=0, tiled=True),
        preferred_element_type=jnp.float32,
    )
    updated = (own_rows.astype(jnp.float32) + rms_norm(projected, post_gain[0])).astype(
        jnp.bfloat16
    )
    closing = rms_norm(updated, final_gain[0]).astype(jnp.bfloat16)
    verdict = jnp.dot(closing, w_judge[0], preferred_element_type=jnp.float32)
    summed_verdict = lax.psum(verdict.astype(jnp.bfloat16), "member").astype(jnp.float32)
    return (updated[None], summed_verdict / lax.axis_size("member"))


def tied(value, *others):
    return lax.optimization_barrier((value, *others))[0]


def call(kernel, out_shape, vmem, **spec):
    return pl.pallas_call(
        kernel,
        out_shape=out_shape,
        compiler_params=pltpu.CompilerParams(vmem_limit_bytes=vmem * MIB),
        cost_estimate=pl.CostEstimate(flops=1000, bytes_accessed=1000, transcendentals=0),
        **spec,
    )


def resident(count):
    return [pl.BlockSpec(memory_space=pltpu.SMEM)] + [
        pl.BlockSpec(memory_space=pltpu.VMEM)
    ] * count


def scalars(count, grid, in_specs, out_specs, scratch=()):
    return dict(
        grid_spec=pltpu.PrefetchScalarGridSpec(
            num_scalar_prefetch=count,
            grid=grid,
            in_specs=in_specs,
            out_specs=out_specs,
            scratch_shapes=scratch,
        )
    )


def halves_kernel(core_ref, q_ref, k_ref, v_ref, mine_ref, other_ref):
    def write(out_ref, core):
        at = 0
        for low in range(core * LANES, q_ref.shape[1], CORES * LANES):
            out_ref[:, at : at + LANES] = q_ref[:, low : low + LANES]
            at += LANES
        for ref in (k_ref, v_ref):
            size = ref.shape[1] // CORES
            out_ref[:, at : at + size] = ref[:, core * size : (core + 1) * size]
            at += size

    for core in range(CORES):

        @pl.when(core_ref[0] == core)
        def _(core=core):
            write(mine_ref, core)
            write(other_ref, 1 - core)


def halves(core, w_query, w_key, w_value):
    rows = w_query.shape[0]
    wide = (w_query.shape[1] + w_key.shape[1] + w_value.shape[1]) // CORES
    whole = lambda array: pl.BlockSpec(array.shape, lambda m, c: (0, 0))
    half = jax.ShapeDtypeStruct((rows, wide), w_query.dtype)
    ins = (w_query, w_key, w_value)
    return call(
        halves_kernel, (half, half), 12,
        **scalars(1, (1,), [whole(a) for a in ins], (whole(half), whole(half))),
    )(core, *ins)


def prepare_kernel(slots_ref, own_ref, mate_ref, gain_ref, *chunk_refs):
    count = slots_ref.shape[0] - 1
    width, rows = own_ref.shape
    depth = width // count

    def write(hidden_ref, half):
        values = hidden_ref[...].astype(jnp.float32)
        mean = jnp.sum(values * values, axis=0, keepdims=True) * (1.0 / width)
        scale = lax.rsqrt(mean + epsilon)
        for j in range(count):
            part = slice(j * depth, (j + 1) * depth)
            normed = hidden_ref[part, :].astype(jnp.float32) * scale * gain_ref[part, :]
            normed = normed.T.astype(jnp.bfloat16)
            slot = slots_ref[j]
            low = 0
            for ref in chunk_refs:
                size = ref.shape[0]

                @pl.when((slot >= low) & (slot < low + size))
                def _(ref=ref, low=low):
                    ref[slot - low, pl.ds(pl.multiple_of(half * rows, LANES), rows), :] = normed

                low += size

    core = slots_ref[count]
    write(own_ref, core)
    write(mate_ref, 1 - core)


def prepare(slots, own, mate, gain, sizes):
    width, rows = own.shape
    depth = width // (slots.shape[0] - 1)
    return call(
        prepare_kernel,
        [jax.ShapeDtypeStruct((n, CORES * rows, depth), jnp.bfloat16) for n in sizes],
        14,
        in_specs=resident(3),
        out_specs=[pl.BlockSpec(memory_space=pltpu.VMEM)] * len(sizes),
    )(slots, own, mate, gain)


def rotated(block, cosine, sine):
    lane = lax.broadcasted_iota(jnp.int32, block.shape, 1)
    half = HD // 2
    other = jnp.where(
        lane % HD < half, pltpu.roll(block, LANES - half, 1), pltpu.roll(block, half, 1)
    )
    return block * cosine + other * sine


def qkv_kernel(shape, first, last, chunks_ref, *refs):
    refs = list(refs)
    take = lambda: refs.pop(0)
    units = [[take() for _ in range(n)] for n in shape]
    acc_ref = None if first else take()
    tables = (take(), take()) if last else None
    out_ref = take()
    wide = out_ref.shape[1]
    keys = KVH * HD // CORES
    step = 2 * keys

    def total_of(at):
        total = None if first else acc_ref[:, pl.ds(at, step)]
        for k, parts in enumerate(units):
            for side in range(CORES):
                cols = pl.ds(at + side * wide, step)
                w = parts[0][:, cols]
                for extra in parts[1:]:
                    w = w + extra[:, cols]
                x = chunks_ref[CORES * k + side]
                part = jnp.dot(x, w, preferred_element_type=jnp.float32)
                total = part if total is None else total + part
        return total

    def finish(at, total, rotate_to, scale):
        for low in range(0, step, LANES):
            block = total[:, low : low + LANES]
            if low < rotate_to:
                block = rotated(block, tables[0][...], tables[1][...])
            if scale is not None:
                block = block * scale
            out_ref[:, pl.ds(at + low, LANES)] = block.astype(jnp.bfloat16)

    whole = wide - step if last else wide

    @pl.loop(0, whole // step)
    def _(n):
        at = pl.multiple_of(n * step, step)
        if last:
            finish(at, total_of(at), step, 1.0 / math.sqrt(HD))
        else:
            out_ref[:, pl.ds(at, step)] = total_of(at)

    if last:
        finish(whole, total_of(whole), keys, None)


def qkv_group(chunks, units, acc, tables):
    rows = chunks.shape[1]
    wide = units[0][0].shape[1] // CORES
    first, last = acc is None, tables is not None
    operands = [chunks] + [part for unit in units for part in unit]
    if not first:
        operands.append(acc)
    if last:
        operands += list(tables)
    return call(
        functools.partial(qkv_kernel, [len(unit) for unit in units], first, last),
        jax.ShapeDtypeStruct((rows, wide), jnp.bfloat16 if last else jnp.float32),
        12,
        in_specs=resident(len(operands))[1:],
        out_specs=pl.BlockSpec(memory_space=pltpu.VMEM),
    )(*operands)


def attend_kernel(core_ref, q_ref, own0_ref, own1_ref, mate0_ref, mate1_ref, seg_q_ref, seg0_ref, seg1_ref, *out_refs):
    out_ref = out_refs[-1]
    rows = q_ref.shape[0]
    count = 2 * rows
    distance = (
        lax.broadcasted_iota(jnp.int32, (count, rows), 1)
        + rows
        - lax.broadcasted_iota(jnp.int32, (count, rows), 0)
    )
    seg_keys = jnp.concatenate([seg0_ref[...], seg1_ref[...]], axis=1)
    seg_keys = jnp.broadcast_to(seg_keys, (rows, count)).T
    allowed = (distance >= 0) & (distance < WINDOW) & (seg_q_ref[...] == seg_keys)
    bias = jnp.where(allowed, 0.0, -1e9)
    own = jnp.concatenate([own0_ref[...], own1_ref[...]], axis=0).astype(jnp.float32)
    mate = jnp.concatenate([mate0_ref[...], mate1_ref[...]], axis=0).astype(jnp.float32)
    is_first = core_ref[0] == 0
    part = KVH // CORES
    sides = [jnp.where(is_first, own, mate), jnp.where(is_first, mate, own)]
    span = QH // KVH // CORES
    for g in range(KVH):
        side, at = sides[g // part], g % part * HD
        key = side[:, at : at + HD].astype(jnp.bfloat16)
        at += part * HD
        value_t = side[:, at : at + HD].T.astype(jnp.bfloat16)
        heads = range(g * span, (g + 1) * span)
        query = jnp.concatenate([q_ref[:, h * HD : (h + 1) * HD] for h in heads], axis=0)
        scores = lax.dot_general(
            key, query, (((1,), (1,)), ((), ())), preferred_element_type=jnp.float32
        )
        parts, totals = [], []
        for k in range(span):
            score = jnp.tanh(scores[:, k * rows : (k + 1) * rows] * (1.0 / softcap))
            expanded = jnp.exp2(score * (softcap / math.log(2.0)) + bias)
            totals.append(jnp.sum(expanded, axis=0, keepdims=True))
            parts.append(expanded.astype(jnp.bfloat16))
        mixed = jnp.dot(
            value_t, jnp.concatenate(parts, axis=1), preferred_element_type=jnp.float32
        )
        for k, h in enumerate(heads):
            result = mixed[:, k * rows : (k + 1) * rows] / totals[k]
            out_ref[h * HD : (h + 1) * HD, :] = result.astype(jnp.bfloat16)


def attend(core, qkv, own, mate, halo, seg_q, seg_keys, prior):
    rows = qkv.shape[0]
    q_wide = QH * HD // CORES
    kv_wide = own.shape[1]
    start = 1 if prior is None else 0
    keys = lambda ahead, column: pl.BlockSpec(
        (WINDOW, kv_wide), lambda m, c: (m + ahead, column)
    )
    segs = lambda ahead: pl.BlockSpec((1, WINDOW), lambda m, c: (0, m + start + ahead))
    if prior is None:
        operands = [own, own, mate, mate]
        specs = [keys(0, 0), keys(1, 0), keys(0, 0), keys(1, 0)]
        steps = rows // WINDOW - 1
    else:
        operands = [halo, own, halo, mate]
        specs = [keys(0, 0), keys(0, 0), keys(0, 1), keys(0, 0)]
        steps = 1
    specs = [
        pl.BlockSpec((WINDOW, q_wide), lambda m, c: (m + start, 0)),
        *specs,
        pl.BlockSpec((1, WINDOW), lambda m, c: (0, m + start)),
        segs(0), segs(1),
    ]
    operands = [qkv, *operands, seg_q, seg_keys, seg_keys]
    aliases = {}
    if prior is not None:
        operands.append(prior)
        specs.append(pl.BlockSpec(memory_space=pl.ANY))
        aliases = {len(operands): 0}
    return call(
        attend_kernel,
        jax.ShapeDtypeStruct((q_wide, rows), jnp.bfloat16),
        12,
        input_output_aliases=aliases,
        **scalars(
            1, (steps,), specs, pl.BlockSpec((q_wide, WINDOW), lambda m, c: (0, m + start))
        ),
    )(core, *operands)


def out_kernel(shape, first, last, ids_ref, attended_ref, *refs):
    refs = list(refs)
    units = [[refs.pop(0) for _ in range(n)] for n in shape]
    acc_ref = None if first else refs.pop(0)
    wide = units[0][0].shape[0]
    half = attended_ref.shape[2] // CORES
    step = wide // 5
    core = ids_ref[len(shape)]
    x = jnp.concatenate([attended_ref[ids_ref[k]] for k in range(len(shape))], axis=0)
    for low in range(0, wide, step):
        rows = slice(low, low + step)
        parts = []
        for unit in units:
            w = unit[0][rows, :]
            for extra in unit[1:]:
                w = w + extra[rows, :]
            parts.append(w)
        total = jnp.dot(jnp.concatenate(parts, axis=1), x, preferred_element_type=jnp.float32)
        if not first:
            total = total + acc_ref[rows, :]
        if last:
            left, right = total[:, :half], total[:, half:]
            refs[0][rows, :] = jnp.where(core == 0, left, right)
            refs[1][rows, :] = jnp.where(core == 0, right, left).astype(jnp.bfloat16)
        else:
            refs[0][rows, :] = total


def project(indices, attended, units, acc, last):
    operands = [attended] + [part for unit in units for part in unit]
    if acc is not None:
        operands.append(acc)
    wide, rows = units[0][0].shape[0], attended.shape[2]
    shape = (wide, rows // CORES)
    out_shape = jax.ShapeDtypeStruct((wide, rows), jnp.float32)
    if last:
        out_shape = (
            jax.ShapeDtypeStruct(shape, jnp.float32), jax.ShapeDtypeStruct(shape, jnp.bfloat16)
        )
    vmem = pl.BlockSpec(memory_space=pltpu.VMEM)
    return call(
        functools.partial(out_kernel, [len(unit) for unit in units], acc is None, last),
        out_shape,
        14,
        in_specs=resident(len(operands)),
        out_specs=(vmem, vmem) if last else vmem,
    )(indices, *operands)


def close_kernel(own_ref, mate_ref, hidden_ref, gains_ref, judge_ref, updated_ref, verdict_ref):
    width = own_ref.shape[0]
    step = width // 5
    parts = [slice(low, low + step) for low in range(0, width, step)]
    total_of = lambda rows: own_ref[rows, :] + mate_ref[rows, :].astype(jnp.float32)
    square = None
    for rows in parts:
        total = total_of(rows)
        part = jnp.sum(total * total, axis=0, keepdims=True)
        square = part if square is None else square + part
    scale = lax.rsqrt(square * (1.0 / width) + epsilon)
    square = None
    for rows in parts:
        updated = hidden_ref[rows, :].astype(jnp.float32) + (
            total_of(rows) * scale * gains_ref[rows, 1:2]
        )
        updated = updated.astype(jnp.bfloat16)
        updated_ref[rows, :] = updated
        updated = updated.astype(jnp.float32)
        part = jnp.sum(updated * updated, axis=0, keepdims=True)
        square = part if square is None else square + part
    scale = lax.rsqrt(square * (1.0 / width) + epsilon)
    closing = updated_ref[...].astype(jnp.float32) * scale * gains_ref[:, 2:3]
    verdict = jnp.dot(
        judge_ref[...], closing.astype(jnp.bfloat16), preferred_element_type=jnp.float32
    )
    verdict_ref[...] = verdict.T.astype(jnp.bfloat16)


def close(own, mate, hidden, gains, judge):
    width, half = own.shape
    return call(
        close_kernel,
        (
            jax.ShapeDtypeStruct((width, half), jnp.bfloat16),
            jax.ShapeDtypeStruct((half, judge.shape[0]), jnp.bfloat16),
        ),
        16,
        in_specs=resident(5)[1:],
        out_specs=(pl.BlockSpec(memory_space=pltpu.VMEM),) * 2,
    )(own, mate, hidden, gains, judge)


def move(block, route):
    return lax.ppermute(block, "seq", route)


class Plane:
    def __init__(self):
        index = lax.axis_index("seq")
        self.core, self.chip = index % CORES, index // CORES
        self.z = self.chip // 2
        ends = lambda z: z in (0, 3)
        middle = lambda z: z in (1, 2)
        self.mate = self.route(lambda z, x, c: (z, x, 1 - c))
        self.x_all = self.route(lambda z, x, c: (z, 1 - x, c))
        self.x_end = self.route(lambda z, x, c: (z, 1 - x, c) if ends(z) else None)
        self.x_mid = self.route(lambda z, x, c: (z, 1 - x, c) if middle(z) else None)
        self.z_pair = self.route(lambda z, x, c: (z ^ 1, x, c))
        self.z_mid = self.route(lambda z, x, c: (3 - z, x, c) if middle(z) else None)
        self.z_out = self.route(lambda z, x, c: (z ^ 1, x, c) if middle(z) else None)
        self.line = [(i, i + CORES) for i in range(4 * 2 * CORES - CORES)]

    @staticmethod
    def route(target):
        route = []
        for i in range(4 * 2 * CORES):
            to = target(i // (2 * CORES), i // CORES % 2, i % CORES)
            if to is not None:
                route.append((i, (to[0] * 2 + to[1]) * CORES + to[2]))
        return route

    def sources(self):
        at_end = (self.z == 0) | (self.z == 3)
        pick = lambda end, mid: jnp.where(at_end, end, mid)
        flips = [0, 1, 2, 3, pick(4, 6), pick(5, 5), pick(6, 4), pick(7, 7)]
        return jnp.stack([self.chip ^ f for f in flips]).astype(jnp.int32)


def planned_body(
    hidden, segments, pre_gain, w_query, w_key, w_value, w_output, post_gain, final_gain, w_judge
):
    p = Plane()
    ids = p.sources()
    core = p.core.astype(jnp.int32)[None]
    hidden_t = hidden[0].T
    width, tok_rows = hidden_t.shape
    shards = lax.axis_size("seq")
    chip_rows = CORES * tok_rows
    row_first = p.chip * chip_rows
    unit_out = w_output[0].T

    mine, other = halves(core, w_query[0], w_key[0], w_value[0])
    unit_in = jnp.concatenate([mine, move(other, p.mate)], axis=1)
    a_side = move(unit_in, p.x_all)
    a_near = move(unit_in, p.z_pair)
    a_inner = move(unit_in, p.z_mid)

    gains = jnp.concatenate([pre_gain, post_gain, final_gain], axis=0).T
    order = jnp.repeat(CORES * ids + p.core, CORES)
    order = order ^ (jnp.arange(shards, dtype=jnp.int32) % CORES)
    slots = jnp.argmax(
        order[None, :] == jnp.arange(shards, dtype=jnp.int32)[:, None], axis=1
    ).astype(jnp.int32)
    mate_t = move(tied(hidden_t, unit_in), p.mate)
    chunks, next_chunks, last_chunks = prepare(
        jnp.concatenate([slots, core]), hidden_t, mate_t, gains[:, :1],
        (shards // 2, shards // 4, shards // 4),
    )

    a_side_near = move(tied(a_near, a_side, chunks), p.x_all)
    a_far = move(tied(a_near, a_side, chunks), p.z_mid)
    a_from_inner = move(tied(a_inner, a_side, chunks), p.z_out)

    o_near = move(tied(unit_out, a_from_inner), p.z_pair)
    o_inner = move(tied(unit_out, a_far), p.z_mid)
    a_round = move(a_from_inner + a_far, p.x_all)
    a_side_inner = move(tied(a_side, a_far), p.z_mid)
    a_from_far = move(tied(a_far, a_from_inner), p.z_out)
    o_side = move(tied(unit_out, a_side_near), p.x_all)
    units = [[unit_in], [a_side], [a_near], [a_side_near]]
    acc = qkv_group(chunks, units, None, None)

    half = HD // 2
    lane = jnp.arange(LANES, dtype=jnp.int32)
    frequency = jnp.exp((lane % half).astype(jnp.float32) * (-2.0 * math.log(rope_base) / HD))
    positions = tied(row_first, a_near) + jnp.arange(chip_rows, dtype=jnp.int32)
    angles = positions.astype(jnp.float32)[:, None] * frequency[None, :]
    tables = (jnp.cos(angles), jnp.where(lane % HD < half, -1.0, 1.0) * jnp.sin(angles))
    seg_all = tied(segments, a_near)
    seg_own = lax.dynamic_slice_in_dim(seg_all, row_first, chip_rows, 0)
    seg_prior = lax.dynamic_slice_in_dim(seg_all, jnp.maximum(row_first - WINDOW, 0), WINDOW, 0)
    seg_prior = jnp.where(p.chip > 0, seg_prior, -1)
    seg_keys = jnp.concatenate([seg_prior, seg_own])[None, :]
    seg_q = seg_own[None, :]
    judge_t = tied(w_judge, a_near)[0].T
    next_chunks, judge_t, seg_q, seg_keys, *tables = lax.optimization_barrier(
        (next_chunks, judge_t, seg_q, seg_keys, *tables)
    )

    done = (acc, o_near, o_inner, o_side, a_round, a_side_inner)
    a_x_fourth = move(tied(a_from_far, *done), p.x_end)
    o_far = move(tied(o_near, a_from_far, *done), p.z_mid)
    o_from_inner = move(tied(o_inner, a_from_far, *done), p.z_out)
    o_x_near = move(tied(o_near, a_from_far, *done), p.x_mid)
    acc = qkv_group(next_chunks, [[a_inner, a_from_inner], [a_round]], acc, None)

    done = (a_x_fourth, o_x_near, acc)
    o_round = move(tied(o_from_inner + o_far, *done), p.x_all)
    o_from_far = move(tied(o_far, *done), p.z_out)
    o_side_inner = move(tied(o_side, *done), p.z_mid)
    units = [[a_far, a_from_far], [a_side_inner, a_x_fourth]]
    qkv = qkv_group(last_chunks, units, acc, tables)
    own_kv = qkv[:, QH * HD // CORES :]
    mate_kv = move(own_kv, p.mate)
    halo = jnp.concatenate([own_kv, mate_kv], axis=1)[chip_rows - WINDOW :]
    halo = move(halo, p.line)

    attended = attend(core, qkv, own_kv, mate_kv, None, seg_q, seg_keys, None)

    done = (o_round, halo)
    o_x_fourth = move(tied(o_from_far, *done), p.x_end)
    o_z_side = move(tied(o_side, o_from_far, *done), p.z_out)
    attended = attend(core, qkv, own_kv, mate_kv, halo, seg_q, seg_keys, attended)
    attended = attended.reshape(shards // CORES, -1, chip_rows)

    units = [[unit_out], [o_side], [o_near], [o_inner, o_from_inner], [o_round], [o_far, o_from_far]]
    acc = project(jnp.concatenate([ids[:3], ids[4:7], core]), attended, units, None, False)
    units = [[o_x_near, o_z_side], [o_side_inner, o_x_fourth]]
    own, mate = project(jnp.concatenate([ids[3:4], ids[7:], core]), attended, units, acc, True)
    updated, verdict = close(own, move(mate, p.mate), hidden_t, gains, judge_t)

    members = lax.axis_size("member")
    summed = verdict.astype(jnp.float32)
    for step in range(1, members):
        ring = [(i, (i + step) % members) for i in range(members)]
        summed = summed + lax.ppermute(verdict, "member", ring).astype(jnp.float32)
    return updated.T[None], summed / members


def solution(mesh):
    across = mesh.shape["member"]
    planned = across == 2 and mesh.shape["seq"] == 4 * across * CORES
    return jax.shard_map(
        planned_body if planned else gathered_body,
        mesh=mesh,
        in_specs=(
            P("member", "seq", None),
            P(),
            P("member", None),
            P("member", "seq", None),
            P("member", "seq", None),
            P("member", "seq", None),
            P("member", "seq", None),
            P("member", None),
            P("member", None),
            P("member", None, None),
        ),
        out_specs=(P("member", "seq", None), P("seq", None)),
        check_vma=False,
    )
```

```python
import functools
import math

import jax
import jax.numpy as jnp
from jax import lax
from jax.experimental import pallas as pl
from jax.experimental.pallas import tpu as pltpu
from jax.sharding import PartitionSpec as P

QH = 32
KVH = 4
HD = 64
WINDOW = 128
CORES = 2
LANES = 128

epsilon = 1e-06
softcap = 50.0
rope_base = 10000.0
MIB = 1024 * 1024


def from_behind(block, axis, distance):
    devices = range(lax.axis_size(axis))
    route = [(i - distance, i) for i in devices if i - distance in devices]
    return lax.ppermute(block, axis, route)


def rms_norm(inputs, scale_gain):
    values = inputs.astype(jnp.float32)
    return (
        values * lax.rsqrt(jnp.mean(values * values, axis=-1, keepdims=True) + epsilon) * scale_gain
    )


def rotate(inputs, positions):
    head_size = inputs.shape[-1]
    half_dim = head_size // 2
    frequency = jnp.exp(
        jnp.arange(half_dim, dtype=jnp.float32) * (-2.0 * math.log(rope_base) / head_size)
    )
    angles = positions.astype(jnp.float32)[:, None] * frequency[None, :]
    cosine_term = jnp.cos(angles)[:, None, :]
    sine_term = jnp.sin(angles)[:, None, :]
    lower_half = inputs[..., :half_dim]
    upper_half = inputs[..., half_dim:]
    return jnp.concatenate(
        [
            lower_half * cosine_term - upper_half * sine_term,
            upper_half * cosine_term + lower_half * sine_term,
        ],
        axis=-1,
    )


def attend_heads(block_queries, block_keys, block_values, seg_query, seg_key):
    query_count = block_queries.shape[0]
    key_count = block_keys.shape[0]
    head_span = QH // KVH * HD
    distance = (
        jnp.arange(query_count, dtype=jnp.int32)[:, None]
        + (key_count - query_count)
        - jnp.arange(key_count, dtype=jnp.int32)[None, :]
    )
    allowed = (distance >= 0) & (distance < WINDOW) & (seg_query[:, None] == seg_key[None, :])

    def one_head(head_index):
        query_head = lax.dynamic_slice_in_dim(
            block_queries, head_index * head_span, head_span, 1
        ).reshape(query_count, QH // KVH, HD)
        key_head = lax.dynamic_slice_in_dim(block_keys, head_index * HD, HD, 1)
        value_head = lax.dynamic_slice_in_dim(block_values, head_index * HD, HD, 1)
        scores = jnp.einsum("qgd,kd->gqk", query_head, key_head, preferred_element_type=jnp.float32)
        scores = softcap * jnp.tanh(scores / softcap)
        expanded = jnp.where(allowed[None], jnp.exp(scores), 0.0)
        weights = (expanded / jnp.sum(expanded, axis=-1, keepdims=True)).astype(jnp.bfloat16)
        head_out = jnp.einsum(
            "gqk,kd->qgd", weights, value_head, preferred_element_type=jnp.float32
        )
        return head_out.astype(jnp.bfloat16).reshape(query_count, head_span)

    per_head = lax.map(one_head, jnp.arange(KVH, dtype=jnp.int32))
    return per_head.transpose(1, 0, 2).reshape(query_count, KVH * head_span)


def gathered_body(
    hidden, segments, pre_gain, w_query, w_key, w_value, w_output, post_gain, final_gain, w_judge
):
    tok_rows = hidden.shape[1]
    dev_index = lax.axis_index("seq")
    row_first = dev_index * tok_rows
    own_rows = hidden[0]
    normed = rms_norm(own_rows, pre_gain[0]).astype(jnp.bfloat16)
    earlier = from_behind(normed[tok_rows - WINDOW :], "seq", 1)
    kv_input = jnp.concatenate([earlier, normed], axis=0)
    kv_count = kv_input.shape[0]
    queries = jnp.dot(
        normed,
        lax.all_gather(w_query[0], "seq", axis=0, tiled=True),
        preferred_element_type=jnp.float32,
    )
    key_rows = jnp.dot(
        kv_input,
        lax.all_gather(w_key[0], "seq", axis=0, tiled=True),
        preferred_element_type=jnp.float32,
    )
    val_rows = jnp.dot(
        kv_input,
        lax.all_gather(w_value[0], "seq", axis=0, tiled=True),
        preferred_element_type=jnp.float32,
    )
    query_positions = row_first + jnp.arange(tok_rows, dtype=jnp.int32)
    key_positions = row_first - (kv_count - tok_rows) + jnp.arange(kv_count, dtype=jnp.int32)
    queries = (
        (rotate(queries.reshape(tok_rows, QH, HD), query_positions) * (1.0 / math.sqrt(HD)))
        .astype(jnp.bfloat16)
        .reshape(tok_rows, QH * HD)
    )
    key_rows = (
        rotate(key_rows.reshape(kv_count, KVH, HD), key_positions)
        .astype(jnp.bfloat16)
        .reshape(kv_count, KVH * HD)
    )
    val_rows = val_rows.astype(jnp.bfloat16)
    seg_own = lax.dynamic_slice_in_dim(segments, row_first, tok_rows, 0)
    seg_prior = lax.dynamic_slice_in_dim(segments, jnp.maximum(row_first - WINDOW, 0), WINDOW, 0)
    seg_prior = jnp.where(dev_index > 0, seg_prior, -1)
    seg_keys = jnp.concatenate([seg_prior, seg_own], axis=0)
    block_rows = min(tok_rows, 512)

    def one_block(block_number):
        return attend_heads(queries, key_rows, val_rows, seg_own, seg_keys)

    attended = lax.map(one_block, jnp.arange(tok_rows // block_rows, dtype=jnp.int32)).reshape(
        tok_rows, QH * HD
    )
    projected = jnp.dot(
        attended,
        lax.all_gather(w_output[0], "seq", axis=0, tiled=True),
        preferred_element_type=jnp.float32,
    )
    updated = (own_rows.astype(jnp.float32) + rms_norm(projected, post_gain[0])).astype(
        jnp.bfloat16
    )
    closing = rms_norm(updated, final_gain[0]).astype(jnp.bfloat16)
    verdict = jnp.dot(closing, w_judge[0], preferred_element_type=jnp.float32)
    summed_verdict = lax.psum(verdict.astype(jnp.bfloat16), "member").astype(jnp.float32)
    return (updated[None], summed_verdict / lax.axis_size("member"))


def tied(value, *others):
    return lax.optimization_barrier((value, *others))[0]


def call(kernel, out_shape, vmem, **spec):
    return pl.pallas_call(
        kernel,
        out_shape=out_shape,
        compiler_params=pltpu.CompilerParams(vmem_limit_bytes=vmem * MIB),
        cost_estimate=pl.CostEstimate(flops=1000, bytes_accessed=1000, transcendentals=0),
        **spec,
    )


def resident(count):
    return [pl.BlockSpec(memory_space=pltpu.SMEM)] + [
        pl.BlockSpec(memory_space=pltpu.VMEM)
    ] * count


def scalars(count, grid, in_specs, out_specs, scratch=()):
    return dict(
        grid_spec=pltpu.PrefetchScalarGridSpec(
            num_scalar_prefetch=count,
            grid=grid,
            in_specs=in_specs,
            out_specs=out_specs,
            scratch_shapes=scratch,
        )
    )


def halves_kernel(core_ref, q_ref, k_ref, v_ref, mine_ref, other_ref):
    def write(out_ref, core):
        at = 0
        for low in range(core * LANES, q_ref.shape[1], CORES * LANES):
            out_ref[:, at : at + LANES] = q_ref[:, low : low + LANES]
            at += LANES
        for ref in (k_ref, v_ref):
            size = ref.shape[1] // CORES
            out_ref[:, at : at + size] = ref[:, core * size : (core + 1) * size]
            at += size

    for core in range(CORES):

        @pl.when(core_ref[0] == core)
        def _(core=core):
            write(mine_ref, core)
            write(other_ref, 1 - core)


def halves(core, w_query, w_key, w_value):
    rows = w_query.shape[0]
    wide = (w_query.shape[1] + w_key.shape[1] + w_value.shape[1]) // CORES
    whole = lambda array: pl.BlockSpec(array.shape, lambda m, c: (0, 0))
    half = jax.ShapeDtypeStruct((rows, wide), w_query.dtype)
    ins = (w_query, w_key, w_value)
    return call(
        halves_kernel, (half, half), 12,
        **scalars(1, (1,), [whole(a) for a in ins], (whole(half), whole(half))),
    )(core, *ins)


def prepare_kernel(slots_ref, own_ref, mate_ref, gain_ref, *chunk_refs):
    count = slots_ref.shape[0] - 1
    width, rows = own_ref.shape
    depth = width // count

    def write(hidden_ref, half):
        values = hidden_ref[...].astype(jnp.float32)
        mean = jnp.sum(values * values, axis=0, keepdims=True) * (1.0 / width)
        scale = lax.rsqrt(mean + epsilon)
        for j in range(count):
            part = slice(j * depth, (j + 1) * depth)
            normed = hidden_ref[part, :].astype(jnp.float32) * scale * gain_ref[part, :]
            normed = normed.T.astype(jnp.bfloat16)
            slot = slots_ref[j]
            low = 0
            for ref in chunk_refs:
                size = ref.shape[0]

                @pl.when((slot >= low) & (slot < low + size))
                def _(ref=ref, low=low):
                    ref[slot - low, pl.ds(pl.multiple_of(half * rows, LANES), rows), :] = normed

                low += size

    core = slots_ref[count]
    write(own_ref, core)
    write(mate_ref, 1 - core)


def prepare(slots, own, mate, gain, sizes):
    width, rows = own.shape
    depth = width // (slots.shape[0] - 1)
    return call(
        prepare_kernel,
        [jax.ShapeDtypeStruct((n, CORES * rows, depth), jnp.bfloat16) for n in sizes],
        14,
        in_specs=resident(3),
        out_specs=[pl.BlockSpec(memory_space=pltpu.VMEM)] * len(sizes),
    )(slots, own, mate, gain)


def rotated(block, cosine, sine):
    lane = lax.broadcasted_iota(jnp.int32, block.shape, 1)
    half = HD // 2
    other = jnp.where(
        lane % HD < half, pltpu.roll(block, LANES - half, 1), pltpu.roll(block, half, 1)
    )
    return block * cosine + other * sine


def qkv_kernel(shape, first, last, chunks_ref, *refs):
    refs = list(refs)
    take = lambda: refs.pop(0)
    units = [[take() for _ in range(n)] for n in shape]
    acc_ref = None if first else take()
    tables = (take(), take()) if last else None
    out_ref = take()
    wide = out_ref.shape[1]
    keys = KVH * HD // CORES
    step = 2 * keys

    def total_of(at):
        total = None if first else acc_ref[:, pl.ds(at, step)]
        for k, parts in enumerate(units):
            for side in range(CORES):
                cols = pl.ds(at + side * wide, step)
                w = parts[0][:, cols]
                for extra in parts[1:]:
                    w = w + extra[:, cols]
                x = chunks_ref[CORES * k + side]
                part = jnp.dot(x, w, preferred_element_type=jnp.float32)
                total = part if total is None else total + part
        return total

    def finish(at, total, rotate_to, scale):
        for low in range(0, step, LANES):
            block = total[:, low : low + LANES]
            if low < rotate_to:
                block = rotated(block, tables[0][...], tables[1][...])
            if scale is not None:
                block = block * scale
            out_ref[:, pl.ds(at + low, LANES)] = block.astype(jnp.bfloat16)

    whole = wide - step if last else wide

    @pl.loop(0, whole // step)
    def _(n):
        at = pl.multiple_of(n * step, step)
        if last:
            finish(at, total_of(at), step, 1.0 / math.sqrt(HD))
        else:
            out_ref[:, pl.ds(at, step)] = total_of(at)

    if last:
        finish(whole, total_of(whole), keys, None)


def qkv_group(chunks, units, acc, tables):
    rows = chunks.shape[1]
    wide = units[0][0].shape[1] // CORES
    first, last = acc is None, tables is not None
    operands = [chunks] + [part for unit in units for part in unit]
    if not first:
        operands.append(acc)
    if last:
        operands += list(tables)
    return call(
        functools.partial(qkv_kernel, [len(unit) for unit in units], first, last),
        jax.ShapeDtypeStruct((rows, wide), jnp.bfloat16 if last else jnp.float32),
        12,
        in_specs=resident(len(operands))[1:],
        out_specs=pl.BlockSpec(memory_space=pltpu.VMEM),
    )(*operands)


def attend_kernel(core_ref, q_ref, own0_ref, own1_ref, mate0_ref, mate1_ref, seg_q_ref, seg0_ref, seg1_ref, *out_refs):
    out_ref = out_refs[-1]
    rows = q_ref.shape[0]
    count = 2 * rows
    distance = (
        lax.broadcasted_iota(jnp.int32, (count, rows), 1)
        + rows
        - lax.broadcasted_iota(jnp.int32, (count, rows), 0)
    )
    seg_keys = jnp.concatenate([seg0_ref[...], seg1_ref[...]], axis=1)
    seg_keys = jnp.broadcast_to(seg_keys, (rows, count)).T
    allowed = (distance >= 0) & (distance < WINDOW) & (seg_q_ref[...] == seg_keys)
    bias = jnp.where(allowed, 0.0, -1e9)
    own = jnp.concatenate([own0_ref[...], own1_ref[...]], axis=0).astype(jnp.float32)
    mate = jnp.concatenate([mate0_ref[...], mate1_ref[...]], axis=0).astype(jnp.float32)
    is_first = core_ref[0] == 0
    part = KVH // CORES
    sides = [jnp.where(is_first, own, mate), jnp.where(is_first, mate, own)]
    span = QH // KVH // CORES
    for g in range(KVH):
        side, at = sides[g // part], g % part * HD
        key = side[:, at : at + HD].astype(jnp.bfloat16)
        at += part * HD
        value_t = side[:, at : at + HD].T.astype(jnp.bfloat16)
        heads = range(g * span, (g + 1) * span)
        query = jnp.concatenate([q_ref[:, h * HD : (h + 1) * HD] for h in heads], axis=0)
        scores = lax.dot_general(
            key, query, (((1,), (1,)), ((), ())), preferred_element_type=jnp.float32
        )
        parts, totals = [], []
        for k in range(span):
            score = jnp.tanh(scores[:, k * rows : (k + 1) * rows] * (1.0 / softcap))
            expanded = jnp.exp2(score * (softcap / math.log(2.0)) + bias)
            totals.append(jnp.sum(expanded, axis=0, keepdims=True))
            parts.append(expanded.astype(jnp.bfloat16))
        mixed = jnp.dot(
            value_t, jnp.concatenate(parts, axis=1), preferred_element_type=jnp.float32
        )
        for k, h in enumerate(heads):
            result = mixed[:, k * rows : (k + 1) * rows] / totals[k]
            out_ref[h * HD : (h + 1) * HD, :] = result.astype(jnp.bfloat16)


def attend(core, qkv, own, mate, halo, seg_q, seg_keys, prior):
    rows = qkv.shape[0]
    q_wide = QH * HD // CORES
    kv_wide = own.shape[1]
    start = 1 if prior is None else 0
    keys = lambda ahead, column: pl.BlockSpec(
        (WINDOW, kv_wide), lambda m, c: (m + ahead, column)
    )
    segs = lambda ahead: pl.BlockSpec((1, WINDOW), lambda m, c: (0, m + start + ahead))
    if prior is None:
        operands = [own, own, mate, mate]
        specs = [keys(0, 0), keys(1, 0), keys(0, 0), keys(1, 0)]
        steps = rows // WINDOW - 1
    else:
        operands = [halo, own, halo, mate]
        specs = [keys(0, 0), keys(0, 0), keys(0, 1), keys(0, 0)]
        steps = 1
    specs = [
        pl.BlockSpec((WINDOW, q_wide), lambda m, c: (m + start, 0)),
        *specs,
        pl.BlockSpec((1, WINDOW), lambda m, c: (0, m + start)),
        segs(0), segs(1),
    ]
    operands = [qkv, *operands, seg_q, seg_keys, seg_keys]
    aliases = {}
    if prior is not None:
        operands.append(prior)
        specs.append(pl.BlockSpec(memory_space=pl.ANY))
        aliases = {len(operands): 0}
    return call(
        attend_kernel,
        jax.ShapeDtypeStruct((q_wide, rows), jnp.bfloat16),
        12,
        input_output_aliases=aliases,
        **scalars(
            1, (steps,), specs, pl.BlockSpec((q_wide, WINDOW), lambda m, c: (0, m + start))
        ),
    )(core, *operands)


def out_kernel(shape, first, last, ids_ref, attended_ref, *refs):
    refs = list(refs)
    units = [[refs.pop(0) for _ in range(n)] for n in shape]
    acc_ref = None if first else refs.pop(0)
    wide = units[0][0].shape[0]
    half = attended_ref.shape[2] // CORES
    step = wide // 5
    core = ids_ref[len(shape)]
    x = jnp.concatenate([attended_ref[ids_ref[k]] for k in range(len(shape))], axis=0)
    for low in range(0, wide, step):
        rows = slice(low, low + step)
        parts = []
        for unit in units:
            w = unit[0][rows, :]
            for extra in unit[1:]:
                w = w + extra[rows, :]
            parts.append(w)
        total = jnp.dot(jnp.concatenate(parts, axis=1), x, preferred_element_type=jnp.float32)
        if not first:
            total = total + acc_ref[rows, :]
        if last:
            left, right = total[:, :half], total[:, half:]
            refs[0][rows, :] = jnp.where(core == 0, left, right)
            refs[1][rows, :] = jnp.where(core == 0, right, left).astype(jnp.bfloat16)
        else:
            refs[0][rows, :] = total


def project(indices, attended, units, acc, last):
    operands = [attended] + [part for unit in units for part in unit]
    if acc is not None:
        operands.append(acc)
    wide, rows = units[0][0].shape[0], attended.shape[2]
    shape = (wide, rows // CORES)
    out_shape = jax.ShapeDtypeStruct((wide, rows), jnp.float32)
    if last:
        out_shape = (
            jax.ShapeDtypeStruct(shape, jnp.float32), jax.ShapeDtypeStruct(shape, jnp.bfloat16)
        )
    vmem = pl.BlockSpec(memory_space=pltpu.VMEM)
    return call(
        functools.partial(out_kernel, [len(unit) for unit in units], acc is None, last),
        out_shape,
        14,
        in_specs=resident(len(operands)),
        out_specs=(vmem, vmem) if last else vmem,
    )(indices, *operands)


def close_kernel(own_ref, mate_ref, hidden_ref, gains_ref, judge_ref, updated_ref, verdict_ref):
    width = own_ref.shape[0]
    step = width // 5
    parts = [slice(low, low + step) for low in range(0, width, step)]
    total_of = lambda rows: own_ref[rows, :] + mate_ref[rows, :].astype(jnp.float32)
    square = None
    for rows in parts:
        total = total_of(rows)
        part = jnp.sum(total * total, axis=0, keepdims=True)
        square = part if square is None else square + part
    scale = lax.rsqrt(square * (1.0 / width) + epsilon)
    square = None
    for rows in parts:
        updated = hidden_ref[rows, :].astype(jnp.float32) + (
            total_of(rows) * scale * gains_ref[rows, 1:2]
        )
        updated = updated.astype(jnp.bfloat16)
        updated_ref[rows, :] = updated
        updated = updated.astype(jnp.float32)
        part = jnp.sum(updated * updated, axis=0, keepdims=True)
        square = part if square is None else square + part
    scale = lax.rsqrt(square * (1.0 / width) + epsilon)
    closing = updated_ref[...].astype(jnp.float32) * scale * gains_ref[:, 2:3]
    verdict = jnp.dot(
        judge_ref[...], closing.astype(jnp.bfloat16), preferred_element_type=jnp.float32
    )
    verdict_ref[...] = verdict.T.astype(jnp.bfloat16)


def close(own, mate, hidden, gains, judge):
    width, half = own.shape
    return call(
        close_kernel,
        (
            jax.ShapeDtypeStruct((width, half), jnp.bfloat16),
            jax.ShapeDtypeStruct((half, judge.shape[0]), jnp.bfloat16),
        ),
        16,
        in_specs=resident(5)[1:],
        out_specs=(pl.BlockSpec(memory_space=pltpu.VMEM),) * 2,
    )(own, mate, hidden, gains, judge)


def move(block, route):
    return lax.ppermute(block, "seq", route)


class Plane:
    def __init__(self):
        index = lax.axis_index("seq")
        self.core, self.chip = index % CORES, index // CORES
        self.z = self.chip // 2
        ends = lambda z: z in (0, 3)
        middle = lambda z: z in (1, 2)
        self.mate = self.route(lambda z, x, c: (z, x, 1 - c))
        self.x_all = self.route(lambda z, x, c: (z, 1 - x, c))
        self.x_end = self.route(lambda z, x, c: (z, 1 - x, c) if ends(z) else None)
        self.x_mid = self.route(lambda z, x, c: (z, 1 - x, c) if middle(z) else None)
        self.z_pair = self.route(lambda z, x, c: (z ^ 1, x, c))
        self.z_mid = self.route(lambda z, x, c: (3 - z, x, c) if middle(z) else None)
        self.z_out = self.route(lambda z, x, c: (z ^ 1, x, c) if middle(z) else None)
        self.line = [(i, i + CORES) for i in range(4 * 2 * CORES - CORES)]

    @staticmethod
    def route(target):
        route = []
        for i in range(4 * 2 * CORES):
            to = target(i // (2 * CORES), i // CORES % 2, i % CORES)
            if to is not None:
                route.append((i, (to[0] * 2 + to[1]) * CORES + to[2]))
        return route

    def sources(self):
        at_end = (self.z == 0) | (self.z == 3)
        pick = lambda end, mid: jnp.where(at_end, end, mid)
        flips = [0, 1, 2, 3, pick(4, 6), pick(5, 5), pick(6, 4), pick(7, 7)]
        return jnp.stack([self.chip ^ f for f in flips]).astype(jnp.int32)


def planned_body(
    hidden, segments, pre_gain, w_query, w_key, w_value, w_output, post_gain, final_gain, w_judge
):
    p = Plane()
    ids = p.sources()
    core = p.core.astype(jnp.int32)[None]
    hidden_t = hidden[0].T
    width, tok_rows = hidden_t.shape
    shards = lax.axis_size("seq")
    chip_rows = CORES * tok_rows
    row_first = p.chip * chip_rows
    unit_out = w_output[0].T

    o_side = move(unit_out, p.x_all)
    o_near = move(unit_out, p.z_pair)
    o_inner = move(unit_out, p.z_mid)
    mate_t = move(hidden_t, p.mate)
    mine, other = halves(core, tied(w_query, mate_t)[0], w_key[0], w_value[0])
    unit_in = jnp.concatenate([mine, move(other, p.mate)], axis=1)
    a_inner = move(tied(unit_in, o_inner), p.z_mid)
    a_near = move(tied(unit_in, o_near), p.z_pair)
    a_side = move(tied(unit_in, o_side), p.x_all)

    gains = jnp.concatenate([pre_gain, post_gain, final_gain], axis=0).T
    order = jnp.repeat(CORES * ids + p.core, CORES)
    order = order ^ (jnp.arange(shards, dtype=jnp.int32) % CORES)
    slots = jnp.argmax(
        order[None, :] == jnp.arange(shards, dtype=jnp.int32)[:, None], axis=1
    ).astype(jnp.int32)
    chunks, next_chunks, last_chunks = prepare(
        jnp.concatenate([slots, core]), hidden_t, mate_t, gains[:, :1],
        (shards // 2, shards // 4, shards // 4),
    )

    a_side_near = move(tied(a_near, a_side, chunks), p.x_all)
    a_far = move(tied(a_near, a_side, chunks), p.z_mid)
    a_from_inner = move(tied(a_inner, a_side, chunks), p.z_out)

    a_round = move(a_from_inner + a_far, p.x_all)
    a_side_inner = move(tied(a_side, a_far), p.z_mid)
    a_from_far = move(tied(a_far, a_from_inner), p.z_out)
    units = [[unit_in], [a_side], [a_near], [a_side_near]]
    acc = qkv_group(chunks, units, None, None)

    half = HD // 2
    lane = jnp.arange(LANES, dtype=jnp.int32)
    frequency = jnp.exp((lane % half).astype(jnp.float32) * (-2.0 * math.log(rope_base) / HD))
    positions = tied(row_first, a_near) + jnp.arange(chip_rows, dtype=jnp.int32)
    angles = positions.astype(jnp.float32)[:, None] * frequency[None, :]
    tables = (jnp.cos(angles), jnp.where(lane % HD < half, -1.0, 1.0) * jnp.sin(angles))
    seg_all = tied(segments, a_near)
    seg_own = lax.dynamic_slice_in_dim(seg_all, row_first, chip_rows, 0)
    seg_prior = lax.dynamic_slice_in_dim(seg_all, jnp.maximum(row_first - WINDOW, 0), WINDOW, 0)
    seg_prior = jnp.where(p.chip > 0, seg_prior, -1)
    seg_keys = jnp.concatenate([seg_prior, seg_own])[None, :]
    seg_q = seg_own[None, :]
    judge_t = tied(w_judge, a_near)[0].T
    next_chunks, judge_t, seg_q, seg_keys, *tables = lax.optimization_barrier(
        (next_chunks, judge_t, seg_q, seg_keys, *tables)
    )

    done = (acc, a_round, a_side_inner)
    a_x_fourth = move(tied(a_from_far, *done), p.x_end)
    o_far = move(tied(o_near, a_from_far, *done), p.z_mid)
    o_from_inner = move(tied(o_inner, a_from_far, *done), p.z_out)
    o_x_near = move(tied(o_near, a_from_far, *done), p.x_mid)
    acc = qkv_group(next_chunks, [[a_inner, a_from_inner], [a_round]], acc, None)

    done = (a_x_fourth, o_x_near, acc)
    o_round = move(tied(o_from_inner + o_far, *done), p.x_all)
    o_from_far = move(tied(o_far, *done), p.z_out)
    o_side_inner = move(tied(o_side, *done), p.z_mid)
    units = [[a_far, a_from_far], [a_side_inner, a_x_fourth]]
    qkv = qkv_group(last_chunks, units, acc, tables)
    own_kv = qkv[:, QH * HD // CORES :]
    mate_kv = move(own_kv, p.mate)
    halo = jnp.concatenate([own_kv, mate_kv], axis=1)[chip_rows - WINDOW :]
    halo = move(halo, p.line)

    attended = attend(core, qkv, own_kv, mate_kv, None, seg_q, seg_keys, None)

    done = (o_round, halo)
    o_x_fourth = move(tied(o_from_far, *done), p.x_end)
    o_z_side = move(tied(o_side, o_from_far, *done), p.z_out)
    attended = attend(core, qkv, own_kv, mate_kv, halo, seg_q, seg_keys, attended)
    attended = attended.reshape(shards // CORES, -1, chip_rows)

    units = [[unit_out], [o_side], [o_near], [o_inner, o_from_inner], [o_round], [o_far, o_from_far]]
    acc = project(jnp.concatenate([ids[:3], ids[4:7], core]), attended, units, None, False)
    units = [[o_x_near, o_z_side], [o_side_inner, o_x_fourth]]
    own, mate = project(jnp.concatenate([ids[3:4], ids[7:], core]), attended, units, acc, True)
    updated, verdict = close(own, move(mate, p.mate), hidden_t, gains, judge_t)

    members = lax.axis_size("member")
    summed = verdict.astype(jnp.float32)
    for step in range(1, members):
        ring = [(i, (i + step) % members) for i in range(members)]
        summed = summed + lax.ppermute(verdict, "member", ring).astype(jnp.float32)
    return updated.T[None], summed / members


def solution(mesh):
    across = mesh.shape["member"]
    planned = across == 2 and mesh.shape["seq"] == 4 * across * CORES
    return jax.shard_map(
        planned_body if planned else gathered_body,
        mesh=mesh,
        in_specs=(
            P("member", "seq", None),
            P(),
            P("member", None),
            P("member", "seq", None),
            P("member", "seq", None),
            P("member", "seq", None),
            P("member", "seq", None),
            P("member", None),
            P("member", None),
            P("member", None, None),
        ),
        out_specs=(P("member", "seq", None), P("seq", None)),
        check_vma=False,
    )
```

```python
import functools
import math

import jax
import jax.numpy as jnp
from jax import lax
from jax.experimental import pallas as pl
from jax.experimental.pallas import tpu as pltpu
from jax.sharding import PartitionSpec as P

QH = 32
KVH = 4
HD = 64
WINDOW = 128
CORES = 2
LANES = 128

epsilon = 1e-06
softcap = 50.0
rope_base = 10000.0
MIB = 1024 * 1024


def from_behind(block, axis, distance):
    devices = range(lax.axis_size(axis))
    route = [(i - distance, i) for i in devices if i - distance in devices]
    return lax.ppermute(block, axis, route)


def rms_norm(inputs, scale_gain):
    values = inputs.astype(jnp.float32)
    return (
        values * lax.rsqrt(jnp.mean(values * values, axis=-1, keepdims=True) + epsilon) * scale_gain
    )


def rotate(inputs, positions):
    head_size = inputs.shape[-1]
    half_dim = head_size // 2
    frequency = jnp.exp(
        jnp.arange(half_dim, dtype=jnp.float32) * (-2.0 * math.log(rope_base) / head_size)
    )
    angles = positions.astype(jnp.float32)[:, None] * frequency[None, :]
    cosine_term = jnp.cos(angles)[:, None, :]
    sine_term = jnp.sin(angles)[:, None, :]
    lower_half = inputs[..., :half_dim]
    upper_half = inputs[..., half_dim:]
    return jnp.concatenate(
        [
            lower_half * cosine_term - upper_half * sine_term,
            upper_half * cosine_term + lower_half * sine_term,
        ],
        axis=-1,
    )


def attend_heads(block_queries, block_keys, block_values, seg_query, seg_key):
    query_count = block_queries.shape[0]
    key_count = block_keys.shape[0]
    head_span = QH // KVH * HD
    distance = (
        jnp.arange(query_count, dtype=jnp.int32)[:, None]
        + (key_count - query_count)
        - jnp.arange(key_count, dtype=jnp.int32)[None, :]
    )
    allowed = (distance >= 0) & (distance < WINDOW) & (seg_query[:, None] == seg_key[None, :])

    def one_head(head_index):
        query_head = lax.dynamic_slice_in_dim(
            block_queries, head_index * head_span, head_span, 1
        ).reshape(query_count, QH // KVH, HD)
        key_head = lax.dynamic_slice_in_dim(block_keys, head_index * HD, HD, 1)
        value_head = lax.dynamic_slice_in_dim(block_values, head_index * HD, HD, 1)
        scores = jnp.einsum("qgd,kd->gqk", query_head, key_head, preferred_element_type=jnp.float32)
        scores = softcap * jnp.tanh(scores / softcap)
        expanded = jnp.where(allowed[None], jnp.exp(scores), 0.0)
        weights = (expanded / jnp.sum(expanded, axis=-1, keepdims=True)).astype(jnp.bfloat16)
        head_out = jnp.einsum(
            "gqk,kd->qgd", weights, value_head, preferred_element_type=jnp.float32
        )
        return head_out.astype(jnp.bfloat16).reshape(query_count, head_span)

    per_head = lax.map(one_head, jnp.arange(KVH, dtype=jnp.int32))
    return per_head.transpose(1, 0, 2).reshape(query_count, KVH * head_span)


def gathered_body(
    hidden, segments, pre_gain, w_query, w_key, w_value, w_output, post_gain, final_gain, w_judge
):
    tok_rows = hidden.shape[1]
    dev_index = lax.axis_index("seq")
    row_first = dev_index * tok_rows
    own_rows = hidden[0]
    normed = rms_norm(own_rows, pre_gain[0]).astype(jnp.bfloat16)
    earlier = from_behind(normed[tok_rows - WINDOW :], "seq", 1)
    kv_input = jnp.concatenate([earlier, normed], axis=0)
    kv_count = kv_input.shape[0]
    queries = jnp.dot(
        normed,
        lax.all_gather(w_query[0], "seq", axis=0, tiled=True),
        preferred_element_type=jnp.float32,
    )
    key_rows = jnp.dot(
        kv_input,
        lax.all_gather(w_key[0], "seq", axis=0, tiled=True),
        preferred_element_type=jnp.float32,
    )
    val_rows = jnp.dot(
        kv_input,
        lax.all_gather(w_value[0], "seq", axis=0, tiled=True),
        preferred_element_type=jnp.float32,
    )
    query_positions = row_first + jnp.arange(tok_rows, dtype=jnp.int32)
    key_positions = row_first - (kv_count - tok_rows) + jnp.arange(kv_count, dtype=jnp.int32)
    queries = (
        (rotate(queries.reshape(tok_rows, QH, HD), query_positions) * (1.0 / math.sqrt(HD)))
        .astype(jnp.bfloat16)
        .reshape(tok_rows, QH * HD)
    )
    key_rows = (
        rotate(key_rows.reshape(kv_count, KVH, HD), key_positions)
        .astype(jnp.bfloat16)
        .reshape(kv_count, KVH * HD)
    )
    val_rows = val_rows.astype(jnp.bfloat16)
    seg_own = lax.dynamic_slice_in_dim(segments, row_first, tok_rows, 0)
    seg_prior = lax.dynamic_slice_in_dim(segments, jnp.maximum(row_first - WINDOW, 0), WINDOW, 0)
    seg_prior = jnp.where(dev_index > 0, seg_prior, -1)
    seg_keys = jnp.concatenate([seg_prior, seg_own], axis=0)
    block_rows = min(tok_rows, 512)

    def one_block(block_number):
        return attend_heads(queries, key_rows, val_rows, seg_own, seg_keys)

    attended = lax.map(one_block, jnp.arange(tok_rows // block_rows, dtype=jnp.int32)).reshape(
        tok_rows, QH * HD
    )
    projected = jnp.dot(
        attended,
        lax.all_gather(w_output[0], "seq", axis=0, tiled=True),
        preferred_element_type=jnp.float32,
    )
    updated = (own_rows.astype(jnp.float32) + rms_norm(projected, post_gain[0])).astype(
        jnp.bfloat16
    )
    closing = rms_norm(updated, final_gain[0]).astype(jnp.bfloat16)
    verdict = jnp.dot(closing, w_judge[0], preferred_element_type=jnp.float32)
    summed_verdict = lax.psum(verdict.astype(jnp.bfloat16), "member").astype(jnp.float32)
    return (updated[None], summed_verdict / lax.axis_size("member"))


def tied(value, *others):
    return lax.optimization_barrier((value, *others))[0]


def call(kernel, out_shape, vmem, **spec):
    return pl.pallas_call(
        kernel,
        out_shape=out_shape,
        compiler_params=pltpu.CompilerParams(vmem_limit_bytes=vmem * MIB),
        cost_estimate=pl.CostEstimate(flops=1000, bytes_accessed=1000, transcendentals=0),
        **spec,
    )


def resident(count):
    return [pl.BlockSpec(memory_space=pltpu.SMEM)] + [
        pl.BlockSpec(memory_space=pltpu.VMEM)
    ] * count


def scalars(count, grid, in_specs, out_specs, scratch=()):
    return dict(
        grid_spec=pltpu.PrefetchScalarGridSpec(
            num_scalar_prefetch=count,
            grid=grid,
            in_specs=in_specs,
            out_specs=out_specs,
            scratch_shapes=scratch,
        )
    )


def halves_kernel(core_ref, q_ref, k_ref, v_ref, mine_ref, other_ref):
    def write(out_ref, core):
        at = 0
        for low in range(core * LANES, q_ref.shape[1], CORES * LANES):
            out_ref[:, at : at + LANES] = q_ref[:, low : low + LANES]
            at += LANES
        for ref in (k_ref, v_ref):
            size = ref.shape[1] // CORES
            out_ref[:, at : at + size] = ref[:, core * size : (core + 1) * size]
            at += size

    for core in range(CORES):

        @pl.when(core_ref[0] == core)
        def _(core=core):
            write(mine_ref, core)
            write(other_ref, 1 - core)


def halves(core, w_query, w_key, w_value):
    rows = w_query.shape[0]
    wide = (w_query.shape[1] + w_key.shape[1] + w_value.shape[1]) // CORES
    whole = lambda array: pl.BlockSpec(array.shape, lambda m, c: (0, 0))
    half = jax.ShapeDtypeStruct((rows, wide), w_query.dtype)
    ins = (w_query, w_key, w_value)
    return call(
        halves_kernel, (half, half), 12,
        **scalars(1, (1,), [whole(a) for a in ins], (whole(half), whole(half))),
    )(core, *ins)


def prepare_kernel(slots_ref, own_ref, mate_ref, gain_ref, *chunk_refs):
    count = slots_ref.shape[0] - 1
    width, rows = own_ref.shape
    depth = width // count

    def write(hidden_ref, half):
        values = hidden_ref[...].astype(jnp.float32)
        mean = jnp.sum(values * values, axis=0, keepdims=True) * (1.0 / width)
        scale = lax.rsqrt(mean + epsilon)
        for j in range(count):
            part = slice(j * depth, (j + 1) * depth)
            normed = hidden_ref[part, :].astype(jnp.float32) * scale * gain_ref[part, :]
            normed = normed.T.astype(jnp.bfloat16)
            slot = slots_ref[j]
            low = 0
            for ref in chunk_refs:
                size = ref.shape[0]

                @pl.when((slot >= low) & (slot < low + size))
                def _(ref=ref, low=low):
                    ref[slot - low, pl.ds(pl.multiple_of(half * rows, LANES), rows), :] = normed

                low += size

    core = slots_ref[count]
    write(own_ref, core)
    write(mate_ref, 1 - core)


def prepare(slots, own, mate, gain, sizes):
    width, rows = own.shape
    depth = width // (slots.shape[0] - 1)
    return call(
        prepare_kernel,
        [jax.ShapeDtypeStruct((n, CORES * rows, depth), jnp.bfloat16) for n in sizes],
        14,
        in_specs=resident(3),
        out_specs=[pl.BlockSpec(memory_space=pltpu.VMEM)] * len(sizes),
    )(slots, own, mate, gain)


def rotated(block, cosine, sine):
    lane = lax.broadcasted_iota(jnp.int32, block.shape, 1)
    half = HD // 2
    other = jnp.where(
        lane % HD < half, pltpu.roll(block, LANES - half, 1), pltpu.roll(block, half, 1)
    )
    return block * cosine + other * sine


def qkv_kernel(shape, first, last, chunks_ref, *refs):
    refs = list(refs)
    take = lambda: refs.pop(0)
    units = [[take() for _ in range(n)] for n in shape]
    acc_ref = None if first else take()
    tables = (take(), take()) if last else None
    out_ref = take()
    wide = out_ref.shape[1]
    keys = KVH * HD // CORES
    step = 2 * keys

    def total_of(at):
        total = None if first else acc_ref[:, pl.ds(at, step)]
        for k, parts in enumerate(units):
            for side in range(CORES):
                x = chunks_ref[CORES * k + side]
                depth = x.shape[1]
                rows, cols = slice(side * depth, (side + 1) * depth), pl.ds(at, step)
                w = parts[0][rows, cols]
                for extra in parts[1:]:
                    w = w + extra[rows, cols]
                part = jnp.dot(x, w, preferred_element_type=jnp.float32)
                total = part if total is None else total + part
        return total

    def finish(at, total, rotate_to, scale):
        for low in range(0, step, LANES):
            block = total[:, low : low + LANES]
            if low < rotate_to:
                block = rotated(block, tables[0][...], tables[1][...])
            if scale is not None:
                block = block * scale
            out_ref[:, pl.ds(at + low, LANES)] = block.astype(jnp.bfloat16)

    whole = wide - step if last else wide

    @pl.loop(0, whole // step)
    def _(n):
        at = pl.multiple_of(n * step, step)
        if last:
            finish(at, total_of(at), step, 1.0 / math.sqrt(HD))
        else:
            out_ref[:, pl.ds(at, step)] = total_of(at)

    if last:
        finish(whole, total_of(whole), keys, None)


def qkv_group(chunks, units, acc, tables):
    rows = chunks.shape[1]
    wide = units[0][0].shape[1]
    first, last = acc is None, tables is not None
    operands = [chunks] + [part for unit in units for part in unit]
    if not first:
        operands.append(acc)
    if last:
        operands += list(tables)
    return call(
        functools.partial(qkv_kernel, [len(unit) for unit in units], first, last),
        jax.ShapeDtypeStruct((rows, wide), jnp.bfloat16 if last else jnp.float32),
        12,
        in_specs=resident(len(operands))[1:],
        out_specs=pl.BlockSpec(memory_space=pltpu.VMEM),
    )(*operands)


def attend_kernel(core_ref, q_ref, own0_ref, own1_ref, mate0_ref, mate1_ref, seg_q_ref, seg0_ref, seg1_ref, *out_refs):
    out_ref = out_refs[-1]
    rows = q_ref.shape[0]
    count = 2 * rows
    distance = (
        lax.broadcasted_iota(jnp.int32, (count, rows), 1)
        + rows
        - lax.broadcasted_iota(jnp.int32, (count, rows), 0)
    )
    seg_keys = jnp.concatenate([seg0_ref[...], seg1_ref[...]], axis=1)
    seg_keys = jnp.broadcast_to(seg_keys, (rows, count)).T
    allowed = (distance >= 0) & (distance < WINDOW) & (seg_q_ref[...] == seg_keys)
    bias = jnp.where(allowed, 0.0, -1e9)
    own = jnp.concatenate([own0_ref[...], own1_ref[...]], axis=0).astype(jnp.float32)
    mate = jnp.concatenate([mate0_ref[...], mate1_ref[...]], axis=0).astype(jnp.float32)
    is_first = core_ref[0] == 0
    part = KVH // CORES
    sides = [jnp.where(is_first, own, mate), jnp.where(is_first, mate, own)]
    span = QH // KVH // CORES
    for g in range(KVH):
        side, at = sides[g // part], g % part * HD
        key = side[:, at : at + HD].astype(jnp.bfloat16)
        at += part * HD
        value_t = side[:, at : at + HD].T.astype(jnp.bfloat16)
        heads = range(g * span, (g + 1) * span)
        query = jnp.concatenate([q_ref[:, h * HD : (h + 1) * HD] for h in heads], axis=0)
        scores = lax.dot_general(
            key, query, (((1,), (1,)), ((), ())), preferred_element_type=jnp.float32
        )
        parts, totals = [], []
        for k in range(span):
            score = jnp.tanh(scores[:, k * rows : (k + 1) * rows] * (1.0 / softcap))
            expanded = jnp.exp2(score * (softcap / math.log(2.0)) + bias)
            totals.append(jnp.sum(expanded, axis=0, keepdims=True))
            parts.append(expanded.astype(jnp.bfloat16))
        mixed = jnp.dot(
            value_t, jnp.concatenate(parts, axis=1), preferred_element_type=jnp.float32
        )
        for k, h in enumerate(heads):
            result = mixed[:, k * rows : (k + 1) * rows] / totals[k]
            out_ref[h * HD : (h + 1) * HD, :] = result.astype(jnp.bfloat16)


def attend(core, qkv, own, mate, halo, seg_q, seg_keys, prior):
    rows = qkv.shape[0]
    q_wide = QH * HD // CORES
    kv_wide = own.shape[1]
    start = 1 if prior is None else 0
    keys = lambda ahead, column: pl.BlockSpec(
        (WINDOW, kv_wide), lambda m, c: (m + ahead, column)
    )
    segs = lambda ahead: pl.BlockSpec((1, WINDOW), lambda m, c: (0, m + start + ahead))
    if prior is None:
        operands = [own, own, mate, mate]
        specs = [keys(0, 0), keys(1, 0), keys(0, 0), keys(1, 0)]
        steps = rows // WINDOW - 1
    else:
        operands = [halo, own, halo, mate]
        specs = [keys(0, 0), keys(0, 0), keys(0, 1), keys(0, 0)]
        steps = 1
    specs = [
        pl.BlockSpec((WINDOW, q_wide), lambda m, c: (m + start, 0)),
        *specs,
        pl.BlockSpec((1, WINDOW), lambda m, c: (0, m + start)),
        segs(0), segs(1),
    ]
    operands = [qkv, *operands, seg_q, seg_keys, seg_keys]
    aliases = {}
    if prior is not None:
        operands.append(prior)
        specs.append(pl.BlockSpec(memory_space=pl.ANY))
        aliases = {len(operands): 0}
    return call(
        attend_kernel,
        jax.ShapeDtypeStruct((q_wide, rows), jnp.bfloat16),
        12,
        input_output_aliases=aliases,
        **scalars(
            1, (steps,), specs, pl.BlockSpec((q_wide, WINDOW), lambda m, c: (0, m + start))
        ),
    )(core, *operands)


def out_kernel(shape, first, last, ids_ref, attended_ref, *refs):
    refs = list(refs)
    units = [[refs.pop(0) for _ in range(n)] for n in shape]
    acc_ref = None if first else refs.pop(0)
    wide = units[0][0].shape[0]
    half = attended_ref.shape[2] // CORES
    step = wide // 5
    core = ids_ref[len(shape)]
    x = jnp.concatenate([attended_ref[ids_ref[k]] for k in range(len(shape))], axis=0)
    for low in range(0, wide, step):
        rows = slice(low, low + step)
        parts = []
        for unit in units:
            w = unit[0][rows, :]
            for extra in unit[1:]:
                w = w + extra[rows, :]
            parts.append(w)
        total = jnp.dot(jnp.concatenate(parts, axis=1), x, preferred_element_type=jnp.float32)
        if not first:
            total = total + acc_ref[rows, :]
        if last:
            left, right = total[:, :half], total[:, half:]
            refs[0][rows, :] = jnp.where(core == 0, left, right)
            refs[1][rows, :] = jnp.where(core == 0, right, left).astype(jnp.bfloat16)
        else:
            refs[0][rows, :] = total


def project(indices, attended, units, acc, last):
    operands = [attended] + [part for unit in units for part in unit]
    if acc is not None:
        operands.append(acc)
    wide, rows = units[0][0].shape[0], attended.shape[2]
    shape = (wide, rows // CORES)
    out_shape = jax.ShapeDtypeStruct((wide, rows), jnp.float32)
    if last:
        out_shape = (
            jax.ShapeDtypeStruct(shape, jnp.float32), jax.ShapeDtypeStruct(shape, jnp.bfloat16)
        )
    vmem = pl.BlockSpec(memory_space=pltpu.VMEM)
    return call(
        functools.partial(out_kernel, [len(unit) for unit in units], acc is None, last),
        out_shape,
        14,
        in_specs=resident(len(operands)),
        out_specs=(vmem, vmem) if last else vmem,
    )(indices, *operands)


def close_kernel(own_ref, mate_ref, hidden_ref, gains_ref, judge_ref, updated_ref, verdict_ref):
    width = own_ref.shape[0]
    step = width // 5
    parts = [slice(low, low + step) for low in range(0, width, step)]
    total_of = lambda rows: own_ref[rows, :] + mate_ref[rows, :].astype(jnp.float32)
    square = None
    for rows in parts:
        total = total_of(rows)
        part = jnp.sum(total * total, axis=0, keepdims=True)
        square = part if square is None else square + part
    scale = lax.rsqrt(square * (1.0 / width) + epsilon)
    square = None
    for rows in parts:
        updated = hidden_ref[rows, :].astype(jnp.float32) + (
            total_of(rows) * scale * gains_ref[rows, 1:2]
        )
        updated = updated.astype(jnp.bfloat16)
        updated_ref[rows, :] = updated
        updated = updated.astype(jnp.float32)
        part = jnp.sum(updated * updated, axis=0, keepdims=True)
        square = part if square is None else square + part
    scale = lax.rsqrt(square * (1.0 / width) + epsilon)
    closing = updated_ref[...].astype(jnp.float32) * scale * gains_ref[:, 2:3]
    verdict = jnp.dot(
        judge_ref[...], closing.astype(jnp.bfloat16), preferred_element_type=jnp.float32
    )
    verdict_ref[...] = verdict.T.astype(jnp.bfloat16)


def close(own, mate, hidden, gains, judge):
    width, half = own.shape
    return call(
        close_kernel,
        (
            jax.ShapeDtypeStruct((width, half), jnp.bfloat16),
            jax.ShapeDtypeStruct((half, judge.shape[0]), jnp.bfloat16),
        ),
        16,
        in_specs=resident(5)[1:],
        out_specs=(pl.BlockSpec(memory_space=pltpu.VMEM),) * 2,
    )(own, mate, hidden, gains, judge)


def move(block, route):
    return lax.ppermute(block, "seq", route)


class Plane:
    def __init__(self):
        index = lax.axis_index("seq")
        self.core, self.chip = index % CORES, index // CORES
        self.z = self.chip // 2
        ends = lambda z: z in (0, 3)
        middle = lambda z: z in (1, 2)
        self.mate = self.route(lambda z, x, c: (z, x, 1 - c))
        self.x_all = self.route(lambda z, x, c: (z, 1 - x, c))
        self.x_end = self.route(lambda z, x, c: (z, 1 - x, c) if ends(z) else None)
        self.x_mid = self.route(lambda z, x, c: (z, 1 - x, c) if middle(z) else None)
        self.z_pair = self.route(lambda z, x, c: (z ^ 1, x, c))
        self.z_mid = self.route(lambda z, x, c: (3 - z, x, c) if middle(z) else None)
        self.z_out = self.route(lambda z, x, c: (z ^ 1, x, c) if middle(z) else None)
        self.line = [(i, i + CORES) for i in range(4 * 2 * CORES - CORES)]

    @staticmethod
    def route(target):
        route = []
        for i in range(4 * 2 * CORES):
            to = target(i // (2 * CORES), i // CORES % 2, i % CORES)
            if to is not None:
                route.append((i, (to[0] * 2 + to[1]) * CORES + to[2]))
        return route

    def sources(self):
        at_end = (self.z == 0) | (self.z == 3)
        pick = lambda end, mid: jnp.where(at_end, end, mid)
        flips = [0, 1, 2, 3, pick(4, 6), pick(5, 5), pick(6, 4), pick(7, 7)]
        return jnp.stack([self.chip ^ f for f in flips]).astype(jnp.int32)


def planned_body(
    hidden, segments, pre_gain, w_query, w_key, w_value, w_output, post_gain, final_gain, w_judge
):
    p = Plane()
    ids = p.sources()
    core = p.core.astype(jnp.int32)[None]
    hidden_t = hidden[0].T
    width, tok_rows = hidden_t.shape
    shards = lax.axis_size("seq")
    chip_rows = CORES * tok_rows
    row_first = p.chip * chip_rows
    unit_out = w_output[0].T

    o_side = move(unit_out, p.x_all)
    o_near = move(unit_out, p.z_pair)
    o_inner = move(unit_out, p.z_mid)
    mate_t = move(hidden_t, p.mate)
    mine, other = halves(core, tied(w_query, mate_t)[0], w_key[0], w_value[0])
    unit_in = jnp.concatenate([mine, move(other, p.mate)], axis=0)
    a_inner = move(tied(unit_in, o_inner), p.z_mid)
    a_near = move(tied(unit_in, o_near), p.z_pair)
    a_side = move(tied(unit_in, o_side), p.x_all)

    gains = jnp.concatenate([pre_gain, post_gain, final_gain], axis=0).T
    order = jnp.repeat(CORES * ids + p.core, CORES)
    order = order ^ (jnp.arange(shards, dtype=jnp.int32) % CORES)
    slots = jnp.argmax(
        order[None, :] == jnp.arange(shards, dtype=jnp.int32)[:, None], axis=1
    ).astype(jnp.int32)
    chunks, next_chunks, last_chunks = prepare(
        jnp.concatenate([slots, core]), hidden_t, mate_t, gains[:, :1],
        (shards // 2, shards // 4, shards // 4),
    )

    a_side_near = move(tied(a_near, a_side, chunks), p.x_all)
    a_far = move(tied(a_near, a_side, chunks), p.z_mid)
    a_from_inner = move(tied(a_inner, a_side, chunks), p.z_out)

    a_round = move(a_from_inner + a_far, p.x_all)
    a_side_inner = move(tied(a_side, a_far), p.z_mid)
    a_from_far = move(tied(a_far, a_from_inner), p.z_out)
    units = [[unit_in], [a_side], [a_near], [a_side_near]]
    acc = qkv_group(chunks, units, None, None)

    half = HD // 2
    lane = jnp.arange(LANES, dtype=jnp.int32)
    frequency = jnp.exp((lane % half).astype(jnp.float32) * (-2.0 * math.log(rope_base) / HD))
    positions = tied(row_first, a_near) + jnp.arange(chip_rows, dtype=jnp.int32)
    angles = positions.astype(jnp.float32)[:, None] * frequency[None, :]
    tables = (jnp.cos(angles), jnp.where(lane % HD < half, -1.0, 1.0) * jnp.sin(angles))
    seg_all = tied(segments, a_near)
    seg_own = lax.dynamic_slice_in_dim(seg_all, row_first, chip_rows, 0)
    seg_prior = lax.dynamic_slice_in_dim(seg_all, jnp.maximum(row_first - WINDOW, 0), WINDOW, 0)
    seg_prior = jnp.where(p.chip > 0, seg_prior, -1)
    seg_keys = jnp.concatenate([seg_prior, seg_own])[None, :]
    seg_q = seg_own[None, :]
    judge_t = tied(w_judge, a_near)[0].T
    next_chunks, judge_t, seg_q, seg_keys, *tables = lax.optimization_barrier(
        (next_chunks, judge_t, seg_q, seg_keys, *tables)
    )

    done = (acc, a_round, a_side_inner)
    a_x_fourth = move(tied(a_from_far, *done), p.x_end)
    o_far = move(tied(o_near, a_from_far, *done), p.z_mid)
    o_from_inner = move(tied(o_inner, a_from_far, *done), p.z_out)
    o_x_near = move(tied(o_near, a_from_far, *done), p.x_mid)
    acc = qkv_group(next_chunks, [[a_inner, a_from_inner], [a_round]], acc, None)

    done = (a_x_fourth, o_x_near, acc)
    o_round = move(tied(o_from_inner + o_far, *done), p.x_all)
    o_from_far = move(tied(o_far, *done), p.z_out)
    units = [[a_far, a_from_far], [a_side_inner, a_x_fourth]]
    qkv = qkv_group(last_chunks, units, acc, tables)
    own_kv = qkv[:, QH * HD // CORES :]
    mate_kv = move(own_kv, p.mate)
    halo = jnp.concatenate([own_kv, mate_kv], axis=1)[chip_rows - WINDOW :]
    halo = move(halo, p.line)

    attended = attend(core, qkv, own_kv, mate_kv, None, seg_q, seg_keys, None)

    done = (o_round, halo)
    o_last = move(tied(o_from_far + o_inner, *done), p.x_all)
    o_z_side = move(tied(o_side, o_from_far, *done), p.z_out)
    attended = attend(core, qkv, own_kv, mate_kv, halo, seg_q, seg_keys, attended)
    attended = attended.reshape(shards // CORES, -1, chip_rows)

    units = [[unit_out], [o_side], [o_near], [o_inner, o_from_inner], [o_round], [o_far, o_from_far]]
    acc = project(jnp.concatenate([ids[:3], ids[4:7], core]), attended, units, None, False)
    units = [[o_x_near, o_z_side], [o_last]]
    own, mate = project(jnp.concatenate([ids[3:4], ids[7:], core]), attended, units, acc, True)
    updated, verdict = close(own, move(mate, p.mate), hidden_t, gains, judge_t)

    members = lax.axis_size("member")
    summed = verdict.astype(jnp.float32)
    for step in range(1, members):
        ring = [(i, (i + step) % members) for i in range(members)]
        summed = summed + lax.ppermute(verdict, "member", ring).astype(jnp.float32)
    return updated.T[None], summed / members


def solution(mesh):
    across = mesh.shape["member"]
    planned = across == 2 and mesh.shape["seq"] == 4 * across * CORES
    return jax.shard_map(
        planned_body if planned else gathered_body,
        mesh=mesh,
        in_specs=(
            P("member", "seq", None),
            P(),
            P("member", None),
            P("member", "seq", None),
            P("member", "seq", None),
            P("member", "seq", None),
            P("member", "seq", None),
            P("member", None),
            P("member", None),
            P("member", None, None),
        ),
        out_specs=(P("member", "seq", None), P("seq", None)),
        check_vma=False,
    )
```

```python
import functools
import math

import jax
import jax.numpy as jnp
from jax import lax
from jax.experimental import pallas as pl
from jax.experimental.pallas import tpu as pltpu
from jax.sharding import PartitionSpec as P

QH = 32
KVH = 4
HD = 64
WINDOW = 128
CORES = 2
LANES = 128

epsilon = 1e-06
softcap = 50.0
rope_base = 10000.0
MIB = 1024 * 1024


def from_behind(block, axis, distance):
    devices = range(lax.axis_size(axis))
    route = [(i - distance, i) for i in devices if i - distance in devices]
    return lax.ppermute(block, axis, route)


def rms_norm(inputs, scale_gain):
    values = inputs.astype(jnp.float32)
    return (
        values * lax.rsqrt(jnp.mean(values * values, axis=-1, keepdims=True) + epsilon) * scale_gain
    )


def rotate(inputs, positions):
    head_size = inputs.shape[-1]
    half_dim = head_size // 2
    frequency = jnp.exp(
        jnp.arange(half_dim, dtype=jnp.float32) * (-2.0 * math.log(rope_base) / head_size)
    )
    angles = positions.astype(jnp.float32)[:, None] * frequency[None, :]
    cosine_term = jnp.cos(angles)[:, None, :]
    sine_term = jnp.sin(angles)[:, None, :]
    lower_half = inputs[..., :half_dim]
    upper_half = inputs[..., half_dim:]
    return jnp.concatenate(
        [
            lower_half * cosine_term - upper_half * sine_term,
            upper_half * cosine_term + lower_half * sine_term,
        ],
        axis=-1,
    )


def attend_heads(block_queries, block_keys, block_values, seg_query, seg_key):
    query_count = block_queries.shape[0]
    key_count = block_keys.shape[0]
    head_span = QH // KVH * HD
    distance = (
        jnp.arange(query_count, dtype=jnp.int32)[:, None]
        + (key_count - query_count)
        - jnp.arange(key_count, dtype=jnp.int32)[None, :]
    )
    allowed = (distance >= 0) & (distance < WINDOW) & (seg_query[:, None] == seg_key[None, :])

    def one_head(head_index):
        query_head = lax.dynamic_slice_in_dim(
            block_queries, head_index * head_span, head_span, 1
        ).reshape(query_count, QH // KVH, HD)
        key_head = lax.dynamic_slice_in_dim(block_keys, head_index * HD, HD, 1)
        value_head = lax.dynamic_slice_in_dim(block_values, head_index * HD, HD, 1)
        scores = jnp.einsum("qgd,kd->gqk", query_head, key_head, preferred_element_type=jnp.float32)
        scores = softcap * jnp.tanh(scores / softcap)
        expanded = jnp.where(allowed[None], jnp.exp(scores), 0.0)
        weights = (expanded / jnp.sum(expanded, axis=-1, keepdims=True)).astype(jnp.bfloat16)
        head_out = jnp.einsum(
            "gqk,kd->qgd", weights, value_head, preferred_element_type=jnp.float32
        )
        return head_out.astype(jnp.bfloat16).reshape(query_count, head_span)

    per_head = lax.map(one_head, jnp.arange(KVH, dtype=jnp.int32))
    return per_head.transpose(1, 0, 2).reshape(query_count, KVH * head_span)


def gathered_body(
    hidden, segments, pre_gain, w_query, w_key, w_value, w_output, post_gain, final_gain, w_judge
):
    tok_rows = hidden.shape[1]
    dev_index = lax.axis_index("seq")
    row_first = dev_index * tok_rows
    own_rows = hidden[0]
    normed = rms_norm(own_rows, pre_gain[0]).astype(jnp.bfloat16)
    earlier = from_behind(normed[tok_rows - WINDOW :], "seq", 1)
    kv_input = jnp.concatenate([earlier, normed], axis=0)
    kv_count = kv_input.shape[0]
    queries = jnp.dot(
        normed,
        lax.all_gather(w_query[0], "seq", axis=0, tiled=True),
        preferred_element_type=jnp.float32,
    )
    key_rows = jnp.dot(
        kv_input,
        lax.all_gather(w_key[0], "seq", axis=0, tiled=True),
        preferred_element_type=jnp.float32,
    )
    val_rows = jnp.dot(
        kv_input,
        lax.all_gather(w_value[0], "seq", axis=0, tiled=True),
        preferred_element_type=jnp.float32,
    )
    query_positions = row_first + jnp.arange(tok_rows, dtype=jnp.int32)
    key_positions = row_first - (kv_count - tok_rows) + jnp.arange(kv_count, dtype=jnp.int32)
    queries = (
        (rotate(queries.reshape(tok_rows, QH, HD), query_positions) * (1.0 / math.sqrt(HD)))
        .astype(jnp.bfloat16)
        .reshape(tok_rows, QH * HD)
    )
    key_rows = (
        rotate(key_rows.reshape(kv_count, KVH, HD), key_positions)
        .astype(jnp.bfloat16)
        .reshape(kv_count, KVH * HD)
    )
    val_rows = val_rows.astype(jnp.bfloat16)
    seg_own = lax.dynamic_slice_in_dim(segments, row_first, tok_rows, 0)
    seg_prior = lax.dynamic_slice_in_dim(segments, jnp.maximum(row_first - WINDOW, 0), WINDOW, 0)
    seg_prior = jnp.where(dev_index > 0, seg_prior, -1)
    seg_keys = jnp.concatenate([seg_prior, seg_own], axis=0)
    block_rows = min(tok_rows, 512)

    def one_block(block_number):
        return attend_heads(queries, key_rows, val_rows, seg_own, seg_keys)

    attended = lax.map(one_block, jnp.arange(tok_rows // block_rows, dtype=jnp.int32)).reshape(
        tok_rows, QH * HD
    )
    projected = jnp.dot(
        attended,
        lax.all_gather(w_output[0], "seq", axis=0, tiled=True),
        preferred_element_type=jnp.float32,
    )
    updated = (own_rows.astype(jnp.float32) + rms_norm(projected, post_gain[0])).astype(
        jnp.bfloat16
    )
    closing = rms_norm(updated, final_gain[0]).astype(jnp.bfloat16)
    verdict = jnp.dot(closing, w_judge[0], preferred_element_type=jnp.float32)
    summed_verdict = lax.psum(verdict.astype(jnp.bfloat16), "member").astype(jnp.float32)
    return (updated[None], summed_verdict / lax.axis_size("member"))


def tied(value, *others):
    return lax.optimization_barrier((value, *others))[0]


def call(kernel, out_shape, vmem, flops=1000, **spec):
    return pl.pallas_call(
        kernel,
        out_shape=out_shape,
        compiler_params=pltpu.CompilerParams(vmem_limit_bytes=vmem * MIB),
        cost_estimate=pl.CostEstimate(flops=flops, bytes_accessed=1000, transcendentals=0),
        **spec,
    )


def resident(count):
    return [pl.BlockSpec(memory_space=pltpu.SMEM)] + [
        pl.BlockSpec(memory_space=pltpu.VMEM)
    ] * count


def scalars(count, grid, in_specs, out_specs, scratch=()):
    return dict(
        grid_spec=pltpu.PrefetchScalarGridSpec(
            num_scalar_prefetch=count,
            grid=grid,
            in_specs=in_specs,
            out_specs=out_specs,
            scratch_shapes=scratch,
        )
    )


def halves_kernel(core_ref, q_ref, k_ref, v_ref, mine_ref, other_ref):
    def write(out_ref, core):
        at = 0
        for low in range(core * LANES, q_ref.shape[1], CORES * LANES):
            out_ref[:, at : at + LANES] = q_ref[:, low : low + LANES]
            at += LANES
        for ref in (k_ref, v_ref):
            size = ref.shape[1] // CORES
            out_ref[:, at : at + size] = ref[:, core * size : (core + 1) * size]
            at += size

    for core in range(CORES):

        @pl.when(core_ref[0] == core)
        def _(core=core):
            write(mine_ref, core)
            write(other_ref, 1 - core)


def halves(core, w_query, w_key, w_value):
    rows = w_query.shape[0]
    wide = (w_query.shape[1] + w_key.shape[1] + w_value.shape[1]) // CORES
    whole = lambda array: pl.BlockSpec(array.shape, lambda m, c: (0, 0))
    half = jax.ShapeDtypeStruct((rows, wide), w_query.dtype)
    ins = (w_query, w_key, w_value)
    return call(
        halves_kernel, (half, half), 12,
        **scalars(1, (1,), [whole(a) for a in ins], (whole(half), whole(half))),
    )(core, *ins)


def prepare_kernel(slots_ref, own_ref, mate_ref, gain_ref, *chunk_refs):
    count = slots_ref.shape[0] - 1
    width, rows = own_ref.shape
    depth = width // count

    def write(hidden_ref, half):
        values = hidden_ref[...].astype(jnp.float32)
        mean = jnp.sum(values * values, axis=0, keepdims=True) * (1.0 / width)
        scale = lax.rsqrt(mean + epsilon)
        for j in range(count):
            part = slice(j * depth, (j + 1) * depth)
            normed = hidden_ref[part, :].astype(jnp.float32) * scale * gain_ref[part, :]
            normed = normed.T.astype(jnp.bfloat16)
            slot = slots_ref[j]
            low = 0
            for ref in chunk_refs:
                size = ref.shape[0]

                @pl.when((slot >= low) & (slot < low + size))
                def _(ref=ref, low=low):
                    ref[slot - low, pl.ds(pl.multiple_of(half * rows, LANES), rows), :] = normed

                low += size

    core = slots_ref[count]
    write(own_ref, core)
    write(mate_ref, 1 - core)


def prepare(slots, own, mate, gain, sizes):
    width, rows = own.shape
    depth = width // (slots.shape[0] - 1)
    return call(
        prepare_kernel,
        [jax.ShapeDtypeStruct((n, CORES * rows, depth), jnp.bfloat16) for n in sizes],
        14,
        in_specs=resident(3),
        out_specs=[pl.BlockSpec(memory_space=pltpu.VMEM)] * len(sizes),
    )(slots, own, mate, gain)


def rotated(block, cosine, sine):
    lane = lax.broadcasted_iota(jnp.int32, block.shape, 1)
    half = HD // 2
    other = jnp.where(
        lane % HD < half, pltpu.roll(block, LANES - half, 1), pltpu.roll(block, half, 1)
    )
    return block * cosine + other * sine


def qkv_kernel(shape, first, last, chunks_ref, *refs):
    refs = list(refs)
    take = lambda: refs.pop(0)
    units = [[take() for _ in range(n)] for n in shape]
    acc_ref = None if first else take()
    tables = (take(), take()) if last else None
    out_ref = take()
    wide = out_ref.shape[1]
    keys = KVH * HD // CORES
    step = 2 * keys

    def total_of(at):
        total = None if first else acc_ref[:, pl.ds(at, step)]
        for k, parts in enumerate(units):
            for side in range(CORES):
                x = chunks_ref[CORES * k + side]
                depth = x.shape[1]
                rows, cols = slice(side * depth, (side + 1) * depth), pl.ds(at, step)
                w = parts[0][rows, cols]
                for extra in parts[1:]:
                    w = w + extra[rows, cols]
                part = jnp.dot(x, w, preferred_element_type=jnp.float32)
                total = part if total is None else total + part
        return total

    def finish(at, total, rotate_to, scale):
        for low in range(0, step, LANES):
            block = total[:, low : low + LANES]
            if low < rotate_to:
                block = rotated(block, tables[0][...], tables[1][...])
            if scale is not None:
                block = block * scale
            out_ref[:, pl.ds(at + low, LANES)] = block.astype(jnp.bfloat16)

    whole = wide - step if last else wide

    @pl.loop(0, whole // step)
    def _(n):
        at = pl.multiple_of(n * step, step)
        if last:
            finish(at, total_of(at), step, 1.0 / math.sqrt(HD))
        else:
            out_ref[:, pl.ds(at, step)] = total_of(at)

    if last:
        finish(whole, total_of(whole), keys, None)


def qkv_group(chunks, units, acc, tables):
    rows = chunks.shape[1]
    wide = units[0][0].shape[1]
    first, last = acc is None, tables is not None
    operands = [chunks] + [part for unit in units for part in unit]
    if not first:
        operands.append(acc)
    if last:
        operands += list(tables)
    return call(
        functools.partial(qkv_kernel, [len(unit) for unit in units], first, last),
        jax.ShapeDtypeStruct((rows, wide), jnp.bfloat16 if last else jnp.float32),
        12,
        in_specs=resident(len(operands))[1:],
        out_specs=pl.BlockSpec(memory_space=pltpu.VMEM),
    )(*operands)


def attend_kernel(core_ref, q_ref, own0_ref, own1_ref, mate0_ref, mate1_ref, seg_q_ref, seg0_ref, seg1_ref, *out_refs):
    out_ref = out_refs[-1]
    rows = q_ref.shape[0]
    count = 2 * rows
    distance = (
        lax.broadcasted_iota(jnp.int32, (count, rows), 1)
        + rows
        - lax.broadcasted_iota(jnp.int32, (count, rows), 0)
    )
    seg_keys = jnp.concatenate([seg0_ref[...], seg1_ref[...]], axis=1)
    seg_keys = jnp.broadcast_to(seg_keys, (rows, count)).T
    allowed = (distance >= 0) & (distance < WINDOW) & (seg_q_ref[...] == seg_keys)
    bias = jnp.where(allowed, 0.0, -1e9)
    own = jnp.concatenate([own0_ref[...], own1_ref[...]], axis=0).astype(jnp.float32)
    mate = jnp.concatenate([mate0_ref[...], mate1_ref[...]], axis=0).astype(jnp.float32)
    is_first = core_ref[0] == 0
    part = KVH // CORES
    sides = [jnp.where(is_first, own, mate), jnp.where(is_first, mate, own)]
    span = QH // KVH // CORES
    for g in range(KVH):
        side, at = sides[g // part], g % part * HD
        key = side[:, at : at + HD].astype(jnp.bfloat16)
        at += part * HD
        value_t = side[:, at : at + HD].T.astype(jnp.bfloat16)
        heads = range(g * span, (g + 1) * span)
        query = jnp.concatenate([q_ref[:, h * HD : (h + 1) * HD] for h in heads], axis=0)
        scores = lax.dot_general(
            key, query, (((1,), (1,)), ((), ())), preferred_element_type=jnp.float32
        )
        parts, totals = [], []
        for k in range(span):
            score = jnp.tanh(scores[:, k * rows : (k + 1) * rows] * (1.0 / softcap))
            expanded = jnp.exp2(score * (softcap / math.log(2.0)) + bias)
            totals.append(jnp.sum(expanded, axis=0, keepdims=True))
            parts.append(expanded.astype(jnp.bfloat16))
        mixed = jnp.dot(
            value_t, jnp.concatenate(parts, axis=1), preferred_element_type=jnp.float32
        )
        for k, h in enumerate(heads):
            result = mixed[:, k * rows : (k + 1) * rows] / totals[k]
            out_ref[h * HD : (h + 1) * HD, :] = result.astype(jnp.bfloat16)


def attend(core, qkv, own, mate, halo, seg_q, seg_keys, prior):
    rows = qkv.shape[0]
    q_wide = QH * HD // CORES
    kv_wide = own.shape[1]
    start = 1 if prior is None else 0
    keys = lambda ahead, column: pl.BlockSpec(
        (WINDOW, kv_wide), lambda m, c: (m + ahead, column)
    )
    segs = lambda ahead: pl.BlockSpec((1, WINDOW), lambda m, c: (0, m + start + ahead))
    if prior is None:
        operands = [own, own, mate, mate]
        specs = [keys(0, 0), keys(1, 0), keys(0, 0), keys(1, 0)]
        steps = rows // WINDOW - 1
    else:
        operands = [halo, own, halo, mate]
        specs = [keys(0, 0), keys(0, 0), keys(0, 1), keys(0, 0)]
        steps = 1
    specs = [
        pl.BlockSpec((WINDOW, q_wide), lambda m, c: (m + start, 0)),
        *specs,
        pl.BlockSpec((1, WINDOW), lambda m, c: (0, m + start)),
        segs(0), segs(1),
    ]
    operands = [qkv, *operands, seg_q, seg_keys, seg_keys]
    aliases = {}
    if prior is not None:
        operands.append(prior)
        specs.append(pl.BlockSpec(memory_space=pl.ANY))
        aliases = {len(operands): 0}
    return call(
        attend_kernel,
        jax.ShapeDtypeStruct((q_wide, rows), jnp.bfloat16),
        12,
        flops=steps * 1600000000,
        input_output_aliases=aliases,
        **scalars(
            1, (steps,), specs, pl.BlockSpec((q_wide, WINDOW), lambda m, c: (0, m + start))
        ),
    )(core, *operands)


def out_kernel(shape, first, side, ids_ref, attended_ref, *refs):
    refs = list(refs)
    units = [[refs.pop(0) for _ in range(n)] for n in shape]
    acc_ref = None if first else refs.pop(0)
    wide = units[0][0].shape[0]
    half = attended_ref.shape[2] // CORES
    step = wide // 5
    lanes = slice(None)
    if side is not None:
        core = ids_ref[len(shape)]
        lanes = pl.ds(pl.multiple_of((core ^ side) * half, LANES), half)
    x = jnp.concatenate([attended_ref[ids_ref[k], :, lanes] for k in range(len(shape))], axis=0)
    for low in range(0, wide, step):
        rows = slice(low, low + step)
        parts = []
        for unit in units:
            w = unit[0][rows, :]
            for extra in unit[1:]:
                w = w + extra[rows, :]
            parts.append(w)
        total = jnp.dot(jnp.concatenate(parts, axis=1), x, preferred_element_type=jnp.float32)
        if not first:
            total = total + acc_ref[rows, lanes]
        refs[0][rows, :] = total.astype(refs[0].dtype)


def project(indices, attended, units, acc, side, dtype):
    operands = [attended] + [part for unit in units for part in unit]
    if acc is not None:
        operands.append(acc)
    wide, rows = units[0][0].shape[0], attended.shape[2]
    return call(
        functools.partial(out_kernel, [len(unit) for unit in units], acc is None, side),
        jax.ShapeDtypeStruct((wide, rows if side is None else rows // CORES), dtype),
        14,
        in_specs=resident(len(operands)),
        out_specs=pl.BlockSpec(memory_space=pltpu.VMEM),
    )(indices, *operands)


def close_kernel(own_ref, mate_ref, hidden_ref, gains_ref, judge_ref, updated_ref, verdict_ref):
    width = own_ref.shape[0]
    step = width // 5
    parts = [slice(low, low + step) for low in range(0, width, step)]
    total_of = lambda rows: own_ref[rows, :] + mate_ref[rows, :].astype(jnp.float32)
    square = None
    for rows in parts:
        total = total_of(rows)
        part = jnp.sum(total * total, axis=0, keepdims=True)
        square = part if square is None else square + part
    scale = lax.rsqrt(square * (1.0 / width) + epsilon)
    square = None
    for rows in parts:
        updated = hidden_ref[rows, :].astype(jnp.float32) + (
            total_of(rows) * scale * gains_ref[rows, 1:2]
        )
        updated = updated.astype(jnp.bfloat16)
        updated_ref[rows, :] = updated
        updated = updated.astype(jnp.float32)
        part = jnp.sum(updated * updated, axis=0, keepdims=True)
        square = part if square is None else square + part
    scale = lax.rsqrt(square * (1.0 / width) + epsilon)
    closing = updated_ref[...].astype(jnp.float32) * scale * gains_ref[:, 2:3]
    verdict = jnp.dot(
        judge_ref[...], closing.astype(jnp.bfloat16), preferred_element_type=jnp.float32
    )
    verdict_ref[...] = verdict.T.astype(jnp.bfloat16)


def close(own, mate, hidden, gains, judge):
    width, half = own.shape
    return call(
        close_kernel,
        (
            jax.ShapeDtypeStruct((width, half), jnp.bfloat16),
            jax.ShapeDtypeStruct((half, judge.shape[0]), jnp.bfloat16),
        ),
        16,
        in_specs=resident(5)[1:],
        out_specs=(pl.BlockSpec(memory_space=pltpu.VMEM),) * 2,
    )(own, mate, hidden, gains, judge)


def move(block, route):
    return lax.ppermute(block, "seq", route)


class Plane:
    def __init__(self):
        index = lax.axis_index("seq")
        self.core, self.chip = index % CORES, index // CORES
        self.z = self.chip // 2
        ends = lambda z: z in (0, 3)
        middle = lambda z: z in (1, 2)
        self.mate = self.route(lambda z, x, c: (z, x, 1 - c))
        self.x_all = self.route(lambda z, x, c: (z, 1 - x, c))
        self.x_end = self.route(lambda z, x, c: (z, 1 - x, c) if ends(z) else None)
        self.x_mid = self.route(lambda z, x, c: (z, 1 - x, c) if middle(z) else None)
        self.z_pair = self.route(lambda z, x, c: (z ^ 1, x, c))
        self.z_mid = self.route(lambda z, x, c: (3 - z, x, c) if middle(z) else None)
        self.z_out = self.route(lambda z, x, c: (z ^ 1, x, c) if middle(z) else None)
        self.line = [(i, i + CORES) for i in range(4 * 2 * CORES - CORES)]

    @staticmethod
    def route(target):
        route = []
        for i in range(4 * 2 * CORES):
            to = target(i // (2 * CORES), i // CORES % 2, i % CORES)
            if to is not None:
                route.append((i, (to[0] * 2 + to[1]) * CORES + to[2]))
        return route

    def sources(self):
        at_end = (self.z == 0) | (self.z == 3)
        pick = lambda end, mid: jnp.where(at_end, end, mid)
        flips = [0, 1, 2, 3, pick(4, 6), pick(5, 5), pick(6, 4), pick(7, 7)]
        return jnp.stack([self.chip ^ f for f in flips]).astype(jnp.int32)


def planned_body(
    hidden, segments, pre_gain, w_query, w_key, w_value, w_output, post_gain, final_gain, w_judge
):
    p = Plane()
    ids = p.sources()
    core = p.core.astype(jnp.int32)[None]
    hidden_t = hidden[0].T
    width, tok_rows = hidden_t.shape
    shards = lax.axis_size("seq")
    chip_rows = CORES * tok_rows
    row_first = p.chip * chip_rows
    unit_out = w_output[0].T

    o_side = move(unit_out, p.x_all)
    o_near = move(unit_out, p.z_pair)
    o_inner = move(unit_out, p.z_mid)
    mate_t = move(hidden_t, p.mate)
    mine, other = halves(core, tied(w_query, mate_t)[0], w_key[0], w_value[0])
    unit_in = jnp.concatenate([mine, move(other, p.mate)], axis=0)
    a_inner = move(tied(unit_in, o_inner), p.z_mid)
    a_near = move(tied(unit_in, o_near), p.z_pair)
    a_side = move(tied(unit_in, o_side), p.x_all)

    gains = jnp.concatenate([pre_gain, post_gain, final_gain], axis=0).T
    order = jnp.repeat(CORES * ids + p.core, CORES)
    order = order ^ (jnp.arange(shards, dtype=jnp.int32) % CORES)
    slots = jnp.argmax(
        order[None, :] == jnp.arange(shards, dtype=jnp.int32)[:, None], axis=1
    ).astype(jnp.int32)
    chunks, next_chunks, last_chunks = prepare(
        jnp.concatenate([slots, core]), hidden_t, mate_t, gains[:, :1],
        (shards // 2, shards // 4, shards // 4),
    )

    a_side_near = move(tied(a_near, a_side, chunks), p.x_all)
    a_far = move(tied(a_near, a_side, chunks), p.z_mid)
    a_from_inner = move(tied(a_inner, a_side, chunks), p.z_out)

    a_round = move(a_from_inner + a_far, p.x_all)
    a_side_inner = move(tied(a_side, a_far), p.z_mid)
    a_from_far = move(tied(a_far, a_from_inner), p.z_out)
    units = [[unit_in], [a_side], [a_near], [a_side_near]]
    acc = qkv_group(chunks, units, None, None)

    half = HD // 2
    lane = jnp.arange(LANES, dtype=jnp.int32)
    frequency = jnp.exp((lane % half).astype(jnp.float32) * (-2.0 * math.log(rope_base) / HD))
    positions = tied(row_first, a_near) + jnp.arange(chip_rows, dtype=jnp.int32)
    angles = positions.astype(jnp.float32)[:, None] * frequency[None, :]
    tables = (jnp.cos(angles), jnp.where(lane % HD < half, -1.0, 1.0) * jnp.sin(angles))
    seg_all = tied(segments, a_near)
    seg_own = lax.dynamic_slice_in_dim(seg_all, row_first, chip_rows, 0)
    seg_prior = lax.dynamic_slice_in_dim(seg_all, jnp.maximum(row_first - WINDOW, 0), WINDOW, 0)
    seg_prior = jnp.where(p.chip > 0, seg_prior, -1)
    seg_keys = jnp.concatenate([seg_prior, seg_own])[None, :]
    seg_q = seg_own[None, :]
    judge_t = tied(w_judge, a_near)[0].T
    next_chunks, judge_t, seg_q, seg_keys, *tables = lax.optimization_barrier(
        (next_chunks, judge_t, seg_q, seg_keys, *tables)
    )

    done = (acc, a_round, a_side_inner)
    a_x_fourth = move(tied(a_from_far, *done), p.x_end)
    o_far = move(tied(o_near, a_from_far, *done), p.z_mid)
    o_from_inner = move(tied(o_inner, a_from_far, *done), p.z_out)
    o_x_near = move(tied(o_near, a_from_far, *done), p.x_mid)
    acc = qkv_group(next_chunks, [[a_inner, a_from_inner], [a_round]], acc, None)

    done = (a_x_fourth, o_x_near, acc)
    o_round = move(tied(o_from_inner + o_far, *done), p.x_all)
    o_from_far = move(tied(o_far, *done), p.z_out)
    units = [[a_far, a_from_far], [a_side_inner, a_x_fourth]]
    qkv = qkv_group(last_chunks, units, acc, tables)
    own_kv = qkv[:, QH * HD // CORES :]
    mate_kv = move(own_kv, p.mate)
    halo = jnp.concatenate([own_kv, mate_kv], axis=1)[chip_rows - WINDOW :]
    halo = move(halo, p.line)

    attended = attend(core, qkv, own_kv, mate_kv, None, seg_q, seg_keys, None)

    done = (o_round, halo)
    o_last = move(tied(o_from_far + o_inner, *done), p.x_all)
    o_z_side = move(tied(o_side, o_from_far, *done), p.z_out)
    attended = attend(core, qkv, own_kv, mate_kv, halo, seg_q, seg_keys, attended)
    attended = attended.reshape(shards // CORES, -1, chip_rows)

    units = [[unit_out], [o_side], [o_near], [o_inner, o_from_inner], [o_round], [o_far, o_from_far]]
    acc = project(jnp.concatenate([ids[:3], ids[4:7], core]), attended, units, None, None, jnp.float32)
    units = [[o_x_near, o_z_side], [o_last]]
    order = jnp.concatenate([ids[3:4], ids[7:], core])
    mate = project(order, attended, units, acc, 1, jnp.bfloat16)
    mate_sum = move(mate, p.mate)
    own = project(order, attended, units, tied(acc, mate), 0, jnp.float32)
    updated, verdict = close(own, mate_sum, hidden_t, gains, judge_t)

    members = lax.axis_size("member")
    summed = verdict.astype(jnp.float32)
    for step in range(1, members):
        ring = [(i, (i + step) % members) for i in range(members)]
        summed = summed + lax.ppermute(verdict, "member", ring).astype(jnp.float32)
    return updated.T[None], summed / members


def solution(mesh):
    across = mesh.shape["member"]
    planned = across == 2 and mesh.shape["seq"] == 4 * across * CORES
    return jax.shard_map(
        planned_body if planned else gathered_body,
        mesh=mesh,
        in_specs=(
            P("member", "seq", None),
            P(),
            P("member", None),
            P("member", "seq", None),
            P("member", "seq", None),
            P("member", "seq", None),
            P("member", "seq", None),
            P("member", None),
            P("member", None),
            P("member", None, None),
        ),
        out_specs=(P("member", "seq", None), P("seq", None)),
        check_vma=False,
    )
```
